128 devices in a mesh: leaf: 32 (over x, y, core), sub: 4 (over z).
Axes of the slice: x: 4, y: 4, z: 4, core: 2. Of those that a mesh axis runs over, the one named last changes fastest.
Arguments:
- right_sides: float32 [16, 128, 1024], P(None, 'leaf', 'sub'), may hold values from -6 to 6
- leaf_order: int32 [128, 1024], P('leaf'), may hold values from 0 to 1023, each once within a row
- leaf_inverse: float32 [128, 1024, 1024], P('leaf', 'sub'), may hold values from -1 to 3
- left_basis: float32 [7, 64, 128, 1024], P(None, None, 'leaf', 'sub'), may hold values from -0.375 to 0.375
- column_factor_bases: float32 [7, 64, 128, 1024], P(None, None, 'leaf', 'sub'), may hold values from -6 to 6
- core_inverse: float32 [128, 128, 128], P('leaf'), may hold values from -1 to 2
Outputs:
- solution: float32 [16, 128, 1024], P(None, 'leaf', 'sub')
The draws below stay inside these ranges and needn't reach their ends.
Inputs may be any that keep to these rules, and one draw needn't show every extreme that they name: `leaf_order`: each row holds every number of 0 to 1023 once.
All inputs are finite; a program needn't handle non-finite values.
Results may differ from the reference program's by a relative error of at most 0.0001.
Values sent between devices are 32-bit elements; how exact they have to be, the bound alone decides.
A program may use at most 64 MiB of HBM per device.

```python
import math
import jax
import jax.numpy as jnp
from jax import lax

MEMBERS = 16
LEAF = 1024
RANK = 64
LEVELS = 7
NL = 128


def dominant_blocks(noise_key, diag_key, count, order, spread, low, high):
    noise = jnp.clip(jax.random.normal(noise_key, (count, order, order), jnp.float32), -4.0, 4.0)
    diagonal = jnp.exp(jax.random.uniform(diag_key, (count, order), jnp.float32, math.log(low), math.log(high)))
    return noise * (spread / math.sqrt(order)) + diagonal[:, :, None] * jnp.eye(order, dtype=jnp.float32)[None]


def draw_leaf_inverse(key, part):
    key = jax.random.fold_in(key, 3)
    first_key, second_key = jax.random.split(key)
    return dominant_blocks(first_key, second_key, NL, LEAF, 0.6, 0.5, 2.0)


def draw_core_inverse(key, part):
    key = jax.random.fold_in(key, 7)
    first_key, second_key = jax.random.split(key)
    return dominant_blocks(first_key, second_key, NL, 2 * RANK, 0.6, 0.3, 1.0)


def level_of(rng, dims, cuts, low, high):
    level, own = 1.0, jax.random.fold_in(rng, 6)
    for dim, blocks in cuts:
        heights = jnp.exp(jax.random.uniform(jax.random.fold_in(own, dim), (blocks,), jnp.float32, low / len(cuts), high / len(cuts)))
        level = level * jnp.repeat(heights, dims[dim] // blocks).reshape([-1 if axis == dim else 1 for axis in range(len(dims))])
    return level


def normal_values(key, shape, scale, bound, cuts=(), kind=jnp.bfloat16):
    gain = level_of(key, shape, cuts, -0.22, 0.18) if cuts else 1.0
    result = jax.random.normal(key, shape, jnp.float32) * scale * gain
    return jnp.minimum(jnp.maximum(result, -bound), bound).astype(kind)


def setup_inputs(seed: int = 0) -> dict:
    seeds = jax.random.split(jax.random.key(seed), 7)
    return {
        "right_sides": normal_values(seeds[0], (MEMBERS, NL, LEAF), 1.0, 6.0, ((1, 32), (2, 4)), jnp.float32),
        "leaf_order": jax.vmap(lambda own: jax.random.permutation(own, LEAF))(jax.random.split(seeds[1], NL)).reshape((NL, LEAF)).astype(jnp.int32),
        "leaf_inverse": draw_leaf_inverse(jax.random.fold_in(seeds[6], 71), 0),
        "left_basis": normal_values(seeds[3], (LEVELS, RANK, NL, LEAF), (4 * RANK) ** -0.5, 0.375, ((2, 32), (3, 4)), jnp.float32),
        "column_factor_bases": normal_values(seeds[4], (LEVELS, RANK, NL, LEAF), 1.0, 6.0, ((2, 32), (3, 4)), jnp.float32),
        "core_inverse": draw_core_inverse(jax.random.fold_in(seeds[6], 71), 0),
    }


def reference(right_sides, leaf_order, leaf_inverse, left_basis, column_factor_bases, core_inverse):
    exact_precision = lax.Precision.HIGHEST
    members, leaves, leaf_size = right_sides.shape
    levels = left_basis.shape[0]
    rank_count = left_basis.shape[1]
    indices = jnp.broadcast_to(leaf_order[None].astype(jnp.int32), right_sides.shape)
    ordered = jnp.take_along_axis(right_sides, indices, axis=2)
    iterate = jnp.einsum('lij,mlj->mli', leaf_inverse, ordered, precision=exact_precision)
    for depth in range(1, levels + 1):
        node_span = 2 ** depth
        half_span = node_span // 2
        groups = leaves // node_span
        norm_factor = 1.0 / math.sqrt(leaf_size * half_span)
        vectors = column_factor_bases[depth - 1].reshape(rank_count, groups, 2, half_span * leaf_size)
        blocks = iterate.reshape(members, groups, 2, half_span * leaf_size)
        projected_values = jnp.einsum('rghp,mghp->gmhr', vectors, blocks, precision=exact_precision) * norm_factor
        stacked_rows = projected_values.reshape(groups, members, 2 * rank_count)
        slot_index = jnp.arange(groups, dtype=jnp.int32) * node_span + half_span - 1
        coupling_block = core_inverse[slot_index]
        solved_rows = jnp.einsum('jyi,jvi->jvy', coupling_block, stacked_rows, precision=exact_precision)
        solved_rows = solved_rows.reshape(groups, members, 2, rank_count)
        bases_up = left_basis[depth - 1].reshape(rank_count, groups, 2, half_span * leaf_size)
        update = jnp.einsum('rghp,gmhr->mghp', bases_up, solved_rows, precision=exact_precision)
        iterate = iterate - update.reshape(members, leaves, leaf_size)
    return iterate
```

```python
import math

import jax
import jax.numpy as jnp
from jax import lax
from jax.experimental import pallas as pl
from jax.experimental.pallas import tpu as pltpu
from jax.sharding import PartitionSpec as P

MESH = pl.DeviceIdType.MESH
f32, bf16 = jnp.float32, jnp.bfloat16

SLOT_LEVELS = (4, 5, 6, 7, 3, 2, 1)
COPIES = 96


def split(value):
    high = value.astype(bf16)
    return high, (value - high.astype(f32)).astype(bf16)


def nt(a, b):
    return lax.dot_general(a, b, (((1,), (1,)), ((), ())), preferred_element_type=f32)


def nn(a, b):
    return lax.dot_general(a, b, (((1,), (0,)), ((), ())), preferred_element_type=f32)


def product(dot, a, b_high, b_low):
    rows = a.shape[0]
    a_high, a_low = split(a)
    both = dot(jnp.concatenate([a_high, a_low], 0), b_high)
    return both[:rows] + both[rows:] + dot(a_high, b_low)


def apply_rows(a, matrix):
    return product(nt, a, *split(matrix))


def kernel(
    right, order, inverse, left, column, cores,
    out,
    rhs, index, inv, u32, v32, core,
    uh, ul, vh, vl,
    q1, q1h, q1l, q3, g21p, g21, rs, g3, ys, g45p, g45, xs, g6p, g6, g3p, ysp, xsp,
    xc, cb, c3,
    field, r1p, r1, r2p, r2, r3p, r3, r4p, r4,
    load_sem, send_sem, recv_sem, c_send, c_recv,
):
    members, leaves, part = right.shape
    leaf, z = lax.axis_index("leaf"), lax.axis_index("sub")
    c = lax.rem(leaf, 2)
    y = lax.rem(lax.div(leaf, 2), 4)
    x = lax.div(leaf, 8)
    me = 2 * z + c
    sibling = (leaf + 1 - 2 * c, z)
    z_peers = [(leaf, lax.rem(z + d, 4)) for d in (1, 2, 3)]
    zc_peers = [(leaf, lax.rem(z + d, 4)) for d in (1, 2, 3)]
    zc_peers += [(leaf + 1 - 2 * c, lax.rem(z + d, 4)) for d in (0, 1, 2, 3)]
    zc_index = [2 * lax.rem(z + d, 4) + c for d in (1, 2, 3)]
    zc_index += [2 * lax.rem(z + d, 4) + 1 - c for d in (0, 1, 2, 3)]
    y_peers = [(8 * x + 2 * lax.rem(y + d, 4) + c, z) for d in (1, 2, 3)]
    x_peers = [(8 * lax.rem(x + d, 4) + 2 * y + c, z) for d in (1, 2, 3)]

    count = [0]
    started = []

    def send(src, dst, device):
        i = count[0]
        count[0] += 1
        copy = pltpu.make_async_remote_copy(
            src_ref=src, dst_ref=dst, send_sem=send_sem.at[i], recv_sem=recv_sem.at[i],
            device_id=device, device_id_type=MESH,
        )
        copy.start()
        started.append(copy)
        return copy

    def receive(copies):
        for copy in copies:
            copy.wait_recv()

    loads = []

    def load(src, dst):
        copy = pltpu.make_async_copy(src, dst, load_sem.at[len(loads)])
        copy.start()
        loads.append(copy)
        return copy

    rhs_loads = [load(right.at[:, l, :], rhs.at[z, l]) for l in range(leaves)]
    order_load = load(order, index)
    basis_loads = [load(column.at[:, :, l, :], v32.at[l]) for l in range(leaves)]
    basis_loads += [load(left.at[:, :, l, :], u32.at[l]) for l in range(leaves)]
    core_load = load(cores, core)
    inverse_loads = [load(inverse.at[l], inv.at[l]) for l in range(leaves)]

    barrier = pltpu.get_barrier_semaphore()
    peers = zc_peers + y_peers + x_peers
    for peer in peers:
        pl.semaphore_signal(barrier, inc=1, device_id=peer, device_id_type=MESH)

    for copy in basis_loads:
        copy.wait()
    for l in range(leaves):
        for slot, level in enumerate(SLOT_LEVELS):
            norm = 1.0 / math.sqrt(1024 * 2 ** (level - 1))
            vh[l, slot], vl[l, slot] = split(v32[l, level - 1] * norm)
        for k in range(7):
            uh[l, k], ul[l, k] = split(u32[l, k])

    def gram(l, slots, levels):
        a_high, a_low = (t[l, slots[0]:slots[1]].reshape(-1, part) for t in (vh, vl))
        b_high, b_low = (t[l, levels[0]:levels[1]].reshape(-1, part) for t in (uh, ul))
        return nt(a_high, b_high) + nt(a_low, b_high) + nt(a_high, b_low)

    low_lanes = lax.broadcasted_iota(jnp.int32, (1, 128), 1) < 64

    def turn(a):
        return pltpu.roll(a, 64, a.ndim - 1)

    def low_low(a, b):
        return jnp.where(low_lanes, a, turn(b))

    def high_high(a, b):
        return jnp.where(low_lanes, turn(a), b)

    for l in range(leaves):
        block = gram(l, (0, 6), (0, 2))
        q1[:, 128 * l : 128 * l + 128] = block
        q1h[:, 128 * l : 128 * l + 128], q1l[:, 128 * l : 128 * l + 128] = split(block)
    for n in range(2):
        g21p[n] = low_low(q1[320:384, 256 * n : 256 * n + 128], q1[320:384, 256 * n + 128 : 256 * n + 256])

    for copy in rhs_loads:
        copy.wait()
    core_load.wait()
    pl.semaphore_wait(barrier, len(peers))
    rhs_copies = [[send(rhs.at[z, l], rhs.at[z, l], peer) for peer in z_peers] for l in range(leaves)]

    last_column = lax.rem(leaf, 8) == 7

    def c_copy(i, j, src, dst, device):
        return pltpu.make_async_remote_copy(
            src_ref=src, dst_ref=dst, send_sem=c_send.at[i], recv_sem=c_recv.at[j],
            device_id=device, device_id_type=MESH,
        )

    along_x = [c_copy(d, d, core.at[3], xc.at[x], x_peers[d]) for d in range(3)]
    along_y_one = [c_copy(3 + d, 3 + y, core.at[3], cb.at[y], y_peers[d]) for d in range(3)]
    along_y_three = [c_copy(6 + d, 6, xc.at[pl.ds(0, 3)], cb.at[pl.ds(3, 3)], y_peers[d]) for d in range(3)]
    to_sibling = c_copy(9, 7, cb, cb, sibling)
    third = c_copy(10, 8, core.at[3], c3, sibling)

    @pl.when(last_column)
    def _():
        for copy in along_x:
            copy.start()
        xc[x] = core[3]

    @pl.when(c == 0)
    def _():
        third.start()
        c3[...] = core[3]

    total = None
    for l in range(leaves):
        block = gram(l, (0, 4), (2, 6))
        total = block if total is None else total + block
    q3[...] = total.reshape(4, 8, 8, 256)
    rs[me] = q3[:, me]
    g21[z] = g21p[...]
    order_load.wait()
    for copy in inverse_loads:
        copy.wait()
    g21_copies = [send(g21p, g21.at[z], peer) for peer in z_peers]
    rs_copies = [send(q3.at[:, i], rs.at[me], peer) for i, peer in zip(zc_index, zc_peers, strict=True)]

    r1_copies = []
    for l in range(leaves):
        receive(rhs_copies[l])
        pieces = []
        for u in range(8):
            place = index[l : l + 1, 128 * u : 128 * u + 128]
            lane = jnp.broadcast_to(place & 127, (members, 128))
            tile = jnp.broadcast_to(place >> 7, (members, 128))
            piece = jnp.zeros((members, 128), f32)
            for t in range(8):
                source = rhs[t // 2, l, :, 128 * (t % 2) : 128 * (t % 2) + 128]
                piece = jnp.where(tile == t, jnp.take_along_axis(source, lane, axis=1), piece)
            pieces.append(piece)
        ordered = jnp.concatenate(pieces, 1)
        values = apply_rows(ordered, inv[l])
        field[l] = values
        r1p[l] = product(nt, values, vh[l, 5:7].reshape(128, part), vl[l, 5:7].reshape(128, part))
        if l % 2 == 1:
            pair = pl.ds(l - 1, 2)
            r1_copies += [send(r1p.at[pair], r1.at[z, pair], peer) for peer in z_peers]
    r1[z] = r1p[...]

    raw = None
    for l in range(leaves):
        block = product(nt, field[l], vh[l, 0:6].reshape(384, part), vl[l, 0:6].reshape(384, part))
        raw = block if raw is None else raw + block

    @pl.when(last_column)
    def _():
        for copy in along_x:
            copy.wait_recv()
        for copy in along_y_three:
            copy.start()
        cb[3:6] = xc[0:3]

    @pl.when(c == 1)
    def _():
        @pl.when(y < 3)
        def _():
            for copy in along_y_one:
                copy.start()
            cb[y] = core[3]

    receive(rs_copies)
    sum_a = rs[0] + rs[2] + rs[4] + rs[6]
    sum_b = rs[1] + rs[3] + rs[5] + rs[7]
    g3p[...] = low_low(sum_a[:, :, :128], sum_b[:, :, :128])
    g3[:, me] = g3p[...]
    ysp[...] = sum_a + sum_b
    ys[y] = ysp[...]
    g3_copies = [send(g3p, g3.at[:, me], peer) for peer in zc_peers]
    ys_copies = [send(ysp, ys.at[y], peer) for peer in y_peers]
    receive(g21_copies)
    coupling = g21[0] + g21[1] + g21[2] + g21[3]
    zeros = jnp.zeros((64, 128), f32)
    coupling = jnp.concatenate(
        [jnp.concatenate([coupling[0], zeros], 1), jnp.concatenate([zeros, coupling[1]], 1)], 0
    )

    receive(r1_copies)
    s = [r1[0, l] + r1[1, l] + r1[2, l] + r1[3, l] for l in range(leaves)]
    s1 = [apply_rows(high_high(s[2 * n], s[2 * n + 1]), core[2 * n]) for n in range(2)]
    p2 = low_low(s[0] + s[1], s[2] + s[3]) - apply_rows(jnp.concatenate(s1, 1), coupling)
    s2 = apply_rows(p2, core[1])
    own = [
        low_low(s1[0], s2),
        jnp.where(low_lanes, turn(s1[0]), turn(s2)),
        jnp.where(low_lanes, s1[1], s2),
        high_high(s1[1], s2),
    ]
    r2p[...] = raw - product(nt, jnp.concatenate(own, 1), q1h[...], q1l[...])
    r2_copies = [send(r2p, r2.at[me], peer) for peer in zc_peers]
    r2[me] = r2p[...]

    def correct(l, coefficients, levels):
        b_high, b_low = (t[l, levels[0]:levels[1]].reshape(-1, part) for t in (uh, ul))
        return product(nn, coefficients, b_high, b_low)

    for l in range(leaves):
        field[l] = field[l] - correct(l, own[l], (0, 2))

    @pl.when(c == 1)
    def _():
        for j in range(3):
            @pl.when(y != j)
            def _():
                c_copy(3, 3 + j, core.at[3], cb.at[j], sibling).wait_recv()

        @pl.when(y != 3)
        def _():
            along_y_three[0].wait_recv()

        to_sibling.start()

    receive(ys_copies)
    for n in range(2):
        g45p[4 * n : 4 * n + 4] = high_high(ys[2 * n, :, :, :128], ys[2 * n + 1, :, :, :128])
    halves = [ys[0, 2:4, :, 128:] + ys[1, 2:4, :, 128:], ys[2, 2:4, :, 128:] + ys[3, 2:4, :, 128:]]
    g45p[8:10] = low_low(halves[0], halves[1])
    xsp[...] = halves[0][1] + halves[1][1]
    g45[:, me] = g45p[...]
    xs[x] = xsp[...]
    xs_copies = [send(xsp, xs.at[x], peer) for peer in x_peers]
    g45_copies = [send(g45p, g45.at[:, me], peer) for peer in zc_peers]

    receive(g3_copies)

    @pl.when(c == 1)
    def _():
        third.wait_recv()

    receive(r2_copies)
    p_a = r2[0] + r2[2] + r2[4] + r2[6]
    p_b = r2[1] + r2[3] + r2[5] + r2[7]
    s3 = apply_rows(low_low(p_a[:, 256:], p_b[:, 256:]), c3[...])
    r3p[...] = p_a[:, :256] + p_b[:, :256] - apply_rows(s3, g3[...].reshape(256, 128))
    r3_copies = [send(r3p, r3.at[y], peer) for peer in y_peers]
    r3[y] = r3p[...]

    receive(xs_copies)
    for n in range(2):
        g6p[n] = high_high(xs[2 * n], xs[2 * n + 1])
    g6[:, me] = g6p[...]
    g6_copies = [send(g6p, g6.at[:, me], peer) for peer in zc_peers]

    @pl.when(c == 0)
    def _():
        to_sibling.wait_recv()

    receive(g45_copies)
    receive(r3_copies)
    s4, below = [], []
    for n in range(2):
        p4 = low_low(r3[2 * n, :, :128], r3[2 * n + 1, :, :128])
        s4.append(apply_rows(p4, cb[2 * n]))
        below.append(r3[2 * n] + r3[2 * n + 1] - apply_rows(s4[n], g45[4 * n : 4 * n + 4].reshape(256, 128)))
    s5 = apply_rows(high_high(below[0][:, :128], below[1][:, :128]), cb[1])
    r4p[...] = below[0][:, 128:] + below[1][:, 128:] - apply_rows(s5, g45[8:10].reshape(128, 128))
    r4_copies = [send(r4p, r4.at[x], peer) for peer in x_peers]
    r4[x] = r4p[...]

    own3 = jnp.where(c == 0, s3, turn(s3))
    own4 = jnp.where(y < 2, s4[0], s4[1])
    own4 = jnp.where(lax.rem(y, 2) == 1, own4, turn(own4))
    own5 = jnp.where(y < 2, s5, turn(s5))
    own34 = jnp.where(low_lanes, own3, own4)
    for l in range(leaves):
        field[l] = field[l] - correct(l, own34, (2, 4)) - correct(l, own5[:, :64], (4, 5))

    receive(g6_copies)
    coupling = jnp.concatenate(
        [
            jnp.concatenate([g6[0].reshape(64, 128), zeros], 1),
            jnp.concatenate([zeros, g6[1].reshape(64, 128)], 1),
        ],
        0,
    )
    receive(r4_copies)
    s6 = [apply_rows(low_low(r4[2 * n], r4[2 * n + 1]), cb[3 + 2 * n]) for n in range(2)]
    p7 = high_high(r4[0] + r4[1], r4[2] + r4[3]) - apply_rows(jnp.concatenate(s6, 1), coupling)
    s7 = apply_rows(p7, cb[4])
    own6 = jnp.where(x < 2, s6[0], s6[1])
    own6 = jnp.where(lax.rem(x, 2) == 0, own6, turn(own6))
    own7 = jnp.where(x < 2, turn(s7), s7)
    own67 = jnp.where(low_lanes, own6, own7)
    for l in range(leaves):
        out[l] = field[l] - correct(l, own67, (5, 7))

    for copy in started:
        copy.wait_send()

    @pl.when(last_column)
    def _():
        for copy in along_x + along_y_three:
            copy.wait_send()

    @pl.when(c == 1)
    def _():
        to_sibling.wait_send()

        @pl.when(y < 3)
        def _():
            for copy in along_y_one:
                copy.wait_send()

    @pl.when(c == 0)
    def _():
        third.wait_send()


def per_device(*inputs):
    members, leaves, part = inputs[0].shape
    size = 4 * part
    vmem = pltpu.VMEM
    scratch = [
        vmem((4, leaves, members, part), f32),
        vmem((leaves, size), jnp.int32),
        vmem((leaves, part, size), f32),
        vmem((leaves, 7, 64, part), f32),
        vmem((leaves, 7, 64, part), f32),
        vmem((leaves, 128, 128), f32),
        vmem((leaves, 7, 64, part), bf16),
        vmem((leaves, 7, 64, part), bf16),
        vmem((leaves, 7, 64, part), bf16),
        vmem((leaves, 7, 64, part), bf16),
        vmem((384, 512), f32),
        vmem((384, 512), bf16),
        vmem((384, 512), bf16),
        vmem((4, 8, 8, 256), f32),
        vmem((2, 64, 128), f32),
        vmem((4, 2, 64, 128), f32),
        vmem((8, 4, 8, 256), f32),
        vmem((4, 8, 8, 128), f32),
        vmem((4, 4, 8, 256), f32),
        vmem((10, 8, 128), f32),
        vmem((10, 8, 8, 128), f32),
        vmem((4, 8, 128), f32),
        vmem((2, 8, 128), f32),
        vmem((2, 8, 8, 128), f32),
        vmem((4, 8, 128), f32),
        vmem((4, 8, 256), f32),
        vmem((8, 128), f32),
        vmem((4, 128, 128), f32),
        vmem((6, 128, 128), f32),
        vmem((128, 128), f32),
        vmem((leaves, members, part), f32),
        vmem((leaves, members, 128), f32),
        vmem((4, leaves, members, 128), f32),
        vmem((members, 384), f32),
        vmem((8, members, 384), f32),
        vmem((members, 256), f32),
        vmem((4, members, 256), f32),
        vmem((members, 128), f32),
        vmem((4, members, 128), f32),
        pltpu.SemaphoreType.DMA((24,)),
        pltpu.SemaphoreType.DMA((COPIES,)),
        pltpu.SemaphoreType.DMA((COPIES,)),
        pltpu.SemaphoreType.DMA((11,)),
        pltpu.SemaphoreType.DMA((9,)),
    ]
    result = pl.pallas_call(
        kernel,
        out_shape=jax.ShapeDtypeStruct((leaves, members, part), f32),
        in_specs=[pl.BlockSpec(memory_space=pl.ANY)] * 6,
        out_specs=pl.BlockSpec(memory_space=pltpu.VMEM),
        scratch_shapes=scratch,
        compiler_params=pltpu.CompilerParams(
            collective_id=0, has_side_effects=True, vmem_limit_bytes=48 * 2**20
        ),
    )(*inputs)
    return jnp.transpose(result, (1, 0, 2))


def solution(mesh):
    in_specs = (
        P(None, "leaf", "sub"),
        P("leaf", None),
        P("leaf", "sub", None),
        P(None, None, "leaf", "sub"),
        P(None, None, "leaf", "sub"),
        P("leaf", None, None),
    )
    return jax.shard_map(
        per_device, mesh=mesh, in_specs=in_specs, out_specs=P(None, "leaf", "sub"), check_vma=False
    )
```

```python
import math

import jax
import jax.numpy as jnp
from jax import lax
from jax.experimental import pallas as pl
from jax.experimental.pallas import tpu as pltpu
from jax.sharding import PartitionSpec as P

MESH = pl.DeviceIdType.MESH
f32, bf16 = jnp.float32, jnp.bfloat16

SLOT_LEVELS = (4, 5, 6, 7, 3, 2, 1)
COPIES = 96


def split(value):
    high = value.astype(bf16)
    return high, (value - high.astype(f32)).astype(bf16)


def nt(a, b):
    return lax.dot_general(a, b, (((1,), (1,)), ((), ())), preferred_element_type=f32)


def nn(a, b):
    return lax.dot_general(a, b, (((1,), (0,)), ((), ())), preferred_element_type=f32)


def product(dot, a, b_high, b_low):
    rows = a.shape[0]
    a_high, a_low = split(a)
    both = dot(jnp.concatenate([a_high, a_low], 0), b_high)
    return both[:rows] + both[rows:] + dot(a_high, b_low)


def apply_rows(a, matrix):
    return product(nt, a, *split(matrix))


def kernel(
    right, order, inverse, left, column, cores,
    out,
    rhs, index, inv, u32, v32, core,
    uh, ul, vh, vl,
    q1, q1h, q1l, q3, g21p, g21, rs, g3, ys, g45p, g45, xs, g6p, g6, g3p, ysp, xsp,
    xc, cb, c3,
    field, r1p, r1, r2p, r2, r3p, r3, r4p, r4,
    load_sem, send_sem, recv_sem, c_send, c_recv,
):
    members, leaves, part = right.shape
    leaf, z = lax.axis_index("leaf"), lax.axis_index("sub")
    c = lax.rem(leaf, 2)
    y = lax.rem(lax.div(leaf, 2), 4)
    x = lax.div(leaf, 8)
    me = 2 * z + c
    sibling = (leaf + 1 - 2 * c, z)
    z_peers = [(leaf, lax.rem(z + d, 4)) for d in (1, 2, 3)]
    zc_peers = [(leaf, lax.rem(z + d, 4)) for d in (1, 2, 3)]
    zc_peers += [(leaf + 1 - 2 * c, lax.rem(z + d, 4)) for d in (0, 1, 2, 3)]
    zc_index = [2 * lax.rem(z + d, 4) + c for d in (1, 2, 3)]
    zc_index += [2 * lax.rem(z + d, 4) + 1 - c for d in (0, 1, 2, 3)]
    y_peers = [(8 * x + 2 * lax.rem(y + d, 4) + c, z) for d in (1, 2, 3)]
    x_peers = [(8 * lax.rem(x + d, 4) + 2 * y + c, z) for d in (1, 2, 3)]

    count = [0]
    started = []

    def send(src, dst, device):
        i = count[0]
        count[0] += 1
        copy = pltpu.make_async_remote_copy(
            src_ref=src, dst_ref=dst, send_sem=send_sem.at[i], recv_sem=recv_sem.at[i],
            device_id=device, device_id_type=MESH,
        )
        copy.start()
        started.append(copy)
        return copy

    def receive(copies):
        for copy in copies:
            copy.wait_recv()

    loads = []

    def load(src, dst):
        copy = pltpu.make_async_copy(src, dst, load_sem.at[len(loads)])
        copy.start()
        loads.append(copy)
        return copy

    rhs_loads = [load(right.at[:, l, :], rhs.at[z, l]) for l in range(leaves)]
    order_load = load(order, index)
    basis_loads = [load(column.at[:, :, l, :], v32.at[l]) for l in range(leaves)]
    basis_loads += [load(left.at[:, :, l, :], u32.at[l]) for l in range(leaves)]
    core_load = load(cores, core)
    inverse_loads = [load(inverse.at[l], inv.at[l]) for l in range(leaves)]

    barrier = pltpu.get_barrier_semaphore()
    peers = zc_peers + y_peers + x_peers
    for peer in peers:
        pl.semaphore_signal(barrier, inc=1, device_id=peer, device_id_type=MESH)

    for copy in basis_loads:
        copy.wait()
    for l in range(leaves):
        for slot, level in enumerate(SLOT_LEVELS):
            norm = 1.0 / math.sqrt(1024 * 2 ** (level - 1))
            vh[l, slot], vl[l, slot] = split(v32[l, level - 1] * norm)
        for k in range(7):
            uh[l, k], ul[l, k] = split(u32[l, k])

    def gram(l, slots, levels):
        a_high, a_low = (t[l, slots[0]:slots[1]].reshape(-1, part) for t in (vh, vl))
        b_high, b_low = (t[l, levels[0]:levels[1]].reshape(-1, part) for t in (uh, ul))
        return nt(a_high, b_high) + nt(a_low, b_high) + nt(a_high, b_low)

    low_lanes = lax.broadcasted_iota(jnp.int32, (1, 128), 1) < 64

    def turn(a):
        return pltpu.roll(a, 64, a.ndim - 1)

    def low_low(a, b):
        return jnp.where(low_lanes, a, turn(b))

    def high_high(a, b):
        return jnp.where(low_lanes, turn(a), b)

    for l in range(leaves):
        block = gram(l, (0, 6), (0, 2))
        q1[:, 128 * l : 128 * l + 128] = block
        q1h[:, 128 * l : 128 * l + 128], q1l[:, 128 * l : 128 * l + 128] = split(block)
    for n in range(2):
        g21p[n] = low_low(q1[320:384, 256 * n : 256 * n + 128], q1[320:384, 256 * n + 128 : 256 * n + 256])

    for copy in rhs_loads:
        copy.wait()
    core_load.wait()
    pl.semaphore_wait(barrier, len(peers))
    rhs_copies = [[send(rhs.at[z, l], rhs.at[z, l], peer) for peer in z_peers] for l in range(leaves)]

    last_column = lax.rem(leaf, 8) == 7

    def c_copy(i, j, src, dst, device):
        return pltpu.make_async_remote_copy(
            src_ref=src, dst_ref=dst, send_sem=c_send.at[i], recv_sem=c_recv.at[j],
            device_id=device, device_id_type=MESH,
        )

    along_x = [c_copy(d, d, core.at[3], xc.at[x], x_peers[d]) for d in range(3)]
    along_y_one = [c_copy(3 + d, 3 + y, core.at[3], cb.at[y], y_peers[d]) for d in range(3)]
    along_y_three = [c_copy(6 + d, 6, xc.at[pl.ds(0, 3)], cb.at[pl.ds(3, 3)], y_peers[d]) for d in range(3)]
    to_sibling = c_copy(9, 7, cb, cb, sibling)
    third = c_copy(10, 8, core.at[3], c3, sibling)

    @pl.when(last_column)
    def _():
        for copy in along_x:
            copy.start()
        xc[x] = core[3]

    @pl.when(c == 0)
    def _():
        third.start()
        c3[...] = core[3]

    total = None
    for l in range(leaves):
        block = gram(l, (0, 4), (2, 6))
        total = block if total is None else total + block
    q3[...] = total.reshape(4, 8, 8, 256)
    rs[me] = q3[:, me]
    g21[z] = g21p[...]
    order_load.wait()
    for copy in inverse_loads:
        copy.wait()
    g21_copies = [send(g21p, g21.at[z], peer) for peer in z_peers]
    rs_copies = [send(q3.at[:, i], rs.at[me], peer) for i, peer in zip(zc_index, zc_peers, strict=True)]

    r1_copies = []
    for l in range(leaves):
        receive(rhs_copies[l])
        pieces = []
        for u in range(8):
            place = index[l : l + 1, 128 * u : 128 * u + 128]
            lane = jnp.broadcast_to(place & 127, (members, 128))
            tile = jnp.broadcast_to(place >> 7, (members, 128))
            piece = jnp.zeros((members, 128), f32)
            for t in range(8):
                source = rhs[t // 2, l, :, 128 * (t % 2) : 128 * (t % 2) + 128]
                piece = jnp.where(tile == t, jnp.take_along_axis(source, lane, axis=1), piece)
            pieces.append(piece)
        ordered = jnp.concatenate(pieces, 1)
        values = apply_rows(ordered, inv[l])
        field[l] = values
        r1p[l] = product(nt, values, vh[l, 5:7].reshape(128, part), vl[l, 5:7].reshape(128, part))
        if l % 2 == 1:
            pair = pl.ds(l - 1, 2)
            r1_copies += [send(r1p.at[pair], r1.at[z, pair], peer) for peer in z_peers]
    r1[z] = r1p[...]

    raw = None
    for l in range(leaves):
        block = product(nt, field[l], vh[l, 0:6].reshape(384, part), vl[l, 0:6].reshape(384, part))
        raw = block if raw is None else raw + block

    @pl.when(last_column)
    def _():
        for copy in along_x:
            copy.wait_recv()
        for copy in along_y_three:
            copy.start()
        cb[3:6] = xc[0:3]

    @pl.when(c == 1)
    def _():
        @pl.when(y < 3)
        def _():
            for copy in along_y_one:
                copy.start()
            cb[y] = core[3]

    receive(rs_copies)
    sum_a = rs[0] + rs[2] + rs[4] + rs[6]
    sum_b = rs[1] + rs[3] + rs[5] + rs[7]
    g3p[...] = low_low(sum_a[:, :, :128], sum_b[:, :, :128])
    g3[:, me] = g3p[...]
    ysp[...] = sum_a + sum_b
    ys[y] = ysp[...]
    g3_copies = [send(g3p, g3.at[:, me], peer) for peer in zc_peers]
    ys_copies = [send(ysp, ys.at[y], peer) for peer in y_peers]
    receive(g21_copies)
    coupling = g21[0] + g21[1] + g21[2] + g21[3]
    zeros = jnp.zeros((64, 128), f32)
    coupling = jnp.concatenate(
        [jnp.concatenate([coupling[0], zeros], 1), jnp.concatenate([zeros, coupling[1]], 1)], 0
    )

    receive(r1_copies)
    s = [r1[0, l] + r1[1, l] + r1[2, l] + r1[3, l] for l in range(leaves)]
    s1 = [apply_rows(high_high(s[2 * n], s[2 * n + 1]), core[2 * n]) for n in range(2)]
    p2 = low_low(s[0] + s[1], s[2] + s[3]) - apply_rows(jnp.concatenate(s1, 1), coupling)
    s2 = apply_rows(p2, core[1])
    own = [
        low_low(s1[0], s2),
        jnp.where(low_lanes, turn(s1[0]), turn(s2)),
        jnp.where(low_lanes, s1[1], s2),
        high_high(s1[1], s2),
    ]
    r2p[...] = raw - product(nt, jnp.concatenate(own, 1), q1h[...], q1l[...])
    r2_copies = [send(r2p, r2.at[me], peer) for peer in zc_peers]
    r2[me] = r2p[...]

    def correct(l, coefficients, levels):
        b_high, b_low = (t[l, levels[0]:levels[1]].reshape(-1, part) for t in (uh, ul))
        return product(nn, coefficients, b_high, b_low)

    for l in range(leaves):
        field[l] = field[l] - correct(l, own[l], (0, 2))

    @pl.when(c == 1)
    def _():
        for j in range(3):
            @pl.when(y != j)
            def _():
                c_copy(3, 3 + j, core.at[3], cb.at[j], sibling).wait_recv()

        @pl.when(y != 3)
        def _():
            along_y_three[0].wait_recv()

        to_sibling.start()

    receive(ys_copies)
    for n in range(2):
        g45p[4 * n : 4 * n + 4] = high_high(ys[2 * n, :, :, :128], ys[2 * n + 1, :, :, :128])
    halves = [ys[0, 2:4, :, 128:] + ys[1, 2:4, :, 128:], ys[2, 2:4, :, 128:] + ys[3, 2:4, :, 128:]]
    g45p[8:10] = low_low(halves[0], halves[1])
    xsp[...] = halves[0][1] + halves[1][1]
    g45[:, me] = g45p[...]
    xs[x] = xsp[...]
    xs_copies = [send(xsp, xs.at[x], peer) for peer in x_peers]
    g45_copies = [send(g45p, g45.at[:, me], peer) for peer in zc_peers]

    receive(g3_copies)

    @pl.when(c == 1)
    def _():
        third.wait_recv()

    receive(r2_copies)
    p_a = r2[0] + r2[2] + r2[4] + r2[6]
    p_b = r2[1] + r2[3] + r2[5] + r2[7]
    s3 = apply_rows(low_low(p_a[:, 256:], p_b[:, 256:]), c3[...])
    r3p[...] = p_a[:, :256] + p_b[:, :256] - apply_rows(s3, g3[...].reshape(256, 128))
    r3_copies = [send(r3p, r3.at[y], peer) for peer in y_peers]
    r3[y] = r3p[...]

    receive(xs_copies)
    for n in range(2):
        g6p[n] = high_high(xs[2 * n], xs[2 * n + 1])
    g6[:, me] = g6p[...]
    g6_copies = [send(g6p, g6.at[:, me], peer) for peer in zc_peers]

    @pl.when(c == 0)
    def _():
        to_sibling.wait_recv()

    receive(g45_copies)
    receive(r3_copies)
    s4, below = [], []
    for n in range(2):
        p4 = low_low(r3[2 * n, :, :128], r3[2 * n + 1, :, :128])
        s4.append(apply_rows(p4, cb[2 * n]))
        below.append(r3[2 * n] + r3[2 * n + 1] - apply_rows(s4[n], g45[4 * n : 4 * n + 4].reshape(256, 128)))
    s5 = apply_rows(high_high(below[0][:, :128], below[1][:, :128]), cb[1])
    r4p[...] = below[0][:, 128:] + below[1][:, 128:] - apply_rows(s5, g45[8:10].reshape(128, 128))
    r4_copies = [send(r4p, r4.at[x], peer) for peer in x_peers]
    r4[x] = r4p[...]

    own3 = jnp.where(c == 0, s3, turn(s3))
    own4 = jnp.where(y < 2, s4[0], s4[1])
    own4 = jnp.where(lax.rem(y, 2) == 1, own4, turn(own4))
    own5 = jnp.where(y < 2, s5, turn(s5))
    own34 = jnp.where(low_lanes, own3, own4)
    for l in range(leaves):
        field[l] = field[l] - correct(l, own34, (2, 4)) - correct(l, own5[:, :64], (4, 5))

    receive(g6_copies)
    coupling = jnp.concatenate(
        [
            jnp.concatenate([g6[0].reshape(64, 128), zeros], 1),
            jnp.concatenate([zeros, g6[1].reshape(64, 128)], 1),
        ],
        0,
    )
    receive(r4_copies)
    s6 = [apply_rows(low_low(r4[2 * n], r4[2 * n + 1]), cb[3 + 2 * n]) for n in range(2)]
    p7 = high_high(r4[0] + r4[1], r4[2] + r4[3]) - apply_rows(jnp.concatenate(s6, 1), coupling)
    s7 = apply_rows(p7, cb[4])
    own6 = jnp.where(x < 2, s6[0], s6[1])
    own6 = jnp.where(lax.rem(x, 2) == 0, own6, turn(own6))
    own7 = jnp.where(x < 2, turn(s7), s7)
    own67 = jnp.where(low_lanes, own6, own7)
    for l in range(leaves):
        out[l] = field[l] - correct(l, own67, (5, 7))

    for copy in started:
        copy.wait_send()

    @pl.when(last_column)
    def _():
        for copy in along_x + along_y_three:
            copy.wait_send()

    @pl.when(c == 1)
    def _():
        to_sibling.wait_send()

        @pl.when(y < 3)
        def _():
            for copy in along_y_one:
                copy.wait_send()

    @pl.when(c == 0)
    def _():
        third.wait_send()


def per_device(*inputs):
    members, leaves, part = inputs[0].shape
    size = 4 * part
    vmem = pltpu.VMEM
    scratch = [
        vmem((4, leaves, members, part), f32),
        vmem((leaves, size), jnp.int32),
        vmem((leaves, part, size), f32),
        vmem((leaves, 7, 64, part), f32),
        vmem((leaves, 7, 64, part), f32),
        vmem((leaves, 128, 128), f32),
        vmem((leaves, 7, 64, part), bf16),
        vmem((leaves, 7, 64, part), bf16),
        vmem((leaves, 7, 64, part), bf16),
        vmem((leaves, 7, 64, part), bf16),
        vmem((384, 512), f32),
        vmem((384, 512), bf16),
        vmem((384, 512), bf16),
        vmem((4, 8, 8, 256), f32),
        vmem((2, 64, 128), f32),
        vmem((4, 2, 64, 128), f32),
        vmem((8, 4, 8, 256), f32),
        vmem((4, 8, 8, 128), f32),
        vmem((4, 4, 8, 256), f32),
        vmem((10, 8, 128), f32),
        vmem((10, 8, 8, 128), f32),
        vmem((4, 8, 128), f32),
        vmem((2, 8, 128), f32),
        vmem((2, 8, 8, 128), f32),
        vmem((4, 8, 128), f32),
        vmem((4, 8, 256), f32),
        vmem((8, 128), f32),
        vmem((4, 128, 128), f32),
        vmem((6, 128, 128), f32),
        vmem((128, 128), f32),
        vmem((leaves, members, part), f32),
        vmem((leaves, members, 128), f32),
        vmem((4, leaves, members, 128), f32),
        vmem((members, 384), f32),
        vmem((8, members, 384), f32),
        vmem((members, 256), f32),
        vmem((4, members, 256), f32),
        vmem((members, 128), f32),
        vmem((4, members, 128), f32),
        pltpu.SemaphoreType.DMA((24,)),
        pltpu.SemaphoreType.DMA((COPIES,)),
        pltpu.SemaphoreType.DMA((COPIES,)),
        pltpu.SemaphoreType.DMA((11,)),
        pltpu.SemaphoreType.DMA((9,)),
    ]
    result = pl.pallas_call(
        kernel,
        out_shape=jax.ShapeDtypeStruct((leaves, members, part), f32),
        in_specs=[pl.BlockSpec(memory_space=pl.ANY)] * 6,
        out_specs=pl.BlockSpec(memory_space=pltpu.VMEM),
        scratch_shapes=scratch,
        compiler_params=pltpu.CompilerParams(
            collective_id=0, has_side_effects=True, vmem_limit_bytes=63 * 2**20
        ),
    )(*inputs)
    return jnp.transpose(result, (1, 0, 2))


def solution(mesh):
    in_specs = (
        P(None, "leaf", "sub"),
        P("leaf", None),
        P("leaf", "sub", None),
        P(None, None, "leaf", "sub"),
        P(None, None, "leaf", "sub"),
        P("leaf", None, None),
    )
    return jax.shard_map(
        per_device, mesh=mesh, in_specs=in_specs, out_specs=P(None, "leaf", "sub"), check_vma=False
    )
```

```python
import math

import jax
import jax.numpy as jnp
from jax import lax
from jax.experimental import pallas as pl
from jax.experimental.pallas import tpu as pltpu
from jax.sharding import PartitionSpec as P

MESH = pl.DeviceIdType.MESH
f32, bf16 = jnp.float32, jnp.bfloat16

SLOT_LEVELS = (4, 5, 6, 7, 3, 2, 1)
STEPS = 16


def split(value):
    high = value.astype(bf16)
    return high, (value - high.astype(f32)).astype(bf16)


def nt(a, b):
    return lax.dot_general(a, b, (((1,), (1,)), ((), ())), preferred_element_type=f32)


def nn(a, b):
    return lax.dot_general(a, b, (((1,), (0,)), ((), ())), preferred_element_type=f32)


def product(dot, a, b_high, b_low):
    rows = a.shape[0]
    a_high, a_low = split(a)
    both = dot(jnp.concatenate([a_high, a_low], 0), b_high)
    return both[:rows] + both[rows:] + dot(a_high, b_low)


def apply_rows(a, matrix):
    return product(nt, a, *split(matrix))


def kernel(
    right, order, inverse, left, column, cores,
    out,
    rhs, index, inv, u32, v32, core,
    uh, ul, vh, vl,
    q1, q1h, q1l, q3, g21p, g21, rs, g3, ys, g45p, g45, xs, g6p, g6, g3p, ysp, xsp,
    xc, cb, c3,
    field, r1p, r1, r2p, r2, r3p, r3, r4p, r4,
    load_sem, send_sem, recv_sem, c_send, c_recv,
):
    members, leaves, part = right.shape
    leaf, z = lax.axis_index("leaf"), lax.axis_index("sub")
    c = lax.rem(leaf, 2)
    y = lax.rem(lax.div(leaf, 2), 4)
    x = lax.div(leaf, 8)
    me = 2 * z + c
    sibling = (leaf + 1 - 2 * c, z)
    z_peers = [(leaf, lax.rem(z + d, 4)) for d in (1, 2, 3)]
    zc_peers = [(leaf, lax.rem(z + d, 4)) for d in (1, 2, 3)]
    zc_peers += [(leaf + 1 - 2 * c, lax.rem(z + d, 4)) for d in (0, 1, 2, 3)]
    zc_index = [2 * lax.rem(z + d, 4) + c for d in (1, 2, 3)]
    zc_index += [2 * lax.rem(z + d, 4) + 1 - c for d in (0, 1, 2, 3)]
    y_peers = [(8 * x + 2 * lax.rem(y + d, 4) + c, z) for d in (1, 2, 3)]
    x_peers = [(8 * lax.rem(x + d, 4) + 2 * y + c, z) for d in (1, 2, 3)]

    steps = []

    def send(parts, landed):
        i = len(steps)
        for src, dst, device in parts:
            remote(send_sem.at[i], recv_sem.at[i], src, dst, device).start()
        steps.append(remote(send_sem.at[i], recv_sem.at[i], landed, landed, sibling))
        return steps[i]

    def remote(sent, received, src, dst, device):
        return pltpu.make_async_remote_copy(
            src_ref=src, dst_ref=dst, send_sem=sent, recv_sem=received,
            device_id=device, device_id_type=MESH,
        )

    loads = []

    def load(parts, landed):
        i = len(loads)
        for src, dst in parts:
            pltpu.make_async_copy(src, dst, load_sem.at[i]).start()
        loads.append(pltpu.make_async_copy(landed, landed, load_sem.at[i]))
        return loads[i]

    rhs_load = load([(right.at[:, l, :], rhs.at[z, l]) for l in range(leaves)], rhs.at[z])
    order_load = load([(order, index)], index)
    column_load = load([(column.at[:, :, l, :], v32.at[l]) for l in range(leaves)], v32)
    left_load = load([(left.at[:, :, l, :], u32.at[l]) for l in range(leaves)], u32)
    core_load = load([(cores, core)], core)
    inverse_load = load([(inverse, inv)], inv)

    barrier = pltpu.get_barrier_semaphore()
    peers = zc_peers + y_peers + x_peers
    for peer in peers:
        pl.semaphore_signal(barrier, inc=1, device_id=peer, device_id_type=MESH)

    column_load.wait()
    left_load.wait()
    for l in range(leaves):
        for slot, level in enumerate(SLOT_LEVELS):
            norm = 1.0 / math.sqrt(1024 * 2 ** (level - 1))
            vh[l, slot], vl[l, slot] = split(v32[l, level - 1] * norm)
        for k in range(7):
            uh[l, k], ul[l, k] = split(u32[l, k])

    def gram(l, slots, levels):
        a_high, a_low = (t[l, slots[0]:slots[1]].reshape(-1, part) for t in (vh, vl))
        b_high, b_low = (t[l, levels[0]:levels[1]].reshape(-1, part) for t in (uh, ul))
        return nt(a_high, b_high) + nt(a_low, b_high) + nt(a_high, b_low)

    low_lanes = lax.broadcasted_iota(jnp.int32, (1, 128), 1) < 64

    def turn(a):
        return pltpu.roll(a, 64, a.ndim - 1)

    def low_low(a, b):
        return jnp.where(low_lanes, a, turn(b))

    def high_high(a, b):
        return jnp.where(low_lanes, turn(a), b)

    for l in range(leaves):
        block = gram(l, (0, 6), (0, 2))
        q1[:, 128 * l : 128 * l + 128] = block
        q1h[:, 128 * l : 128 * l + 128], q1l[:, 128 * l : 128 * l + 128] = split(block)
    for n in range(2):
        g21p[n] = low_low(q1[320:384, 256 * n : 256 * n + 128], q1[320:384, 256 * n + 128 : 256 * n + 256])

    rhs_load.wait()
    core_load.wait()
    pl.semaphore_wait(barrier, len(peers))
    three = pl.ds(0, 3)
    seven = pl.ds(0, 7)
    rhs_steps = [
        send([(rhs.at[z, l], rhs.at[z, l], peer) for peer in z_peers], rhs.at[three, l])
        for l in range(leaves)
    ]

    last_column = lax.rem(leaf, 8) == 7

    def core_copies(i, parts):
        return [remote(c_send.at[i], c_recv.at[i], *each) for each in parts]

    along_x = core_copies(0, [(core.at[3], xc.at[x], peer) for peer in x_peers])
    along_y_one = core_copies(1, [(core.at[3], cb.at[y], peer) for peer in y_peers])
    along_y_three = core_copies(1, [(xc.at[three], cb.at[pl.ds(3, 3)], peer) for peer in y_peers])
    to_sibling = remote(c_send.at[2], c_recv.at[2], cb, cb, sibling)
    third = remote(c_send.at[3], c_recv.at[3], core.at[3], c3, sibling)

    def core_wait(i, landed):
        return remote(c_send.at[i], c_recv.at[i], landed, landed, sibling)

    @pl.when(last_column)
    def _():
        for copy in along_x:
            copy.start()
        xc[x] = core[3]

    @pl.when(c == 0)
    def _():
        third.start()
        c3[...] = core[3]

    total = None
    for l in range(leaves):
        block = gram(l, (0, 4), (2, 6))
        total = block if total is None else total + block
    q3[...] = total.reshape(4, 8, 8, 256)
    rs[me] = q3[:, me]
    g21[z] = g21p[...]
    order_load.wait()
    inverse_load.wait()
    g21_step = send([(g21p, g21.at[z], peer) for peer in z_peers], g21.at[three])
    rs_step = send(
        [(q3.at[:, i], rs.at[me], peer) for i, peer in zip(zc_index, zc_peers, strict=True)],
        rs.at[seven],
    )

    r1_steps = []
    for l in range(leaves):
        rhs_steps[l].wait_recv()
        pieces = []
        for u in range(8):
            place = index[l : l + 1, 128 * u : 128 * u + 128]
            lane = jnp.broadcast_to(place & 127, (members, 128))
            tile = jnp.broadcast_to(place >> 7, (members, 128))
            piece = jnp.zeros((members, 128), f32)
            for t in range(8):
                source = rhs[t // 2, l, :, 128 * (t % 2) : 128 * (t % 2) + 128]
                piece = jnp.where(tile == t, jnp.take_along_axis(source, lane, axis=1), piece)
            pieces.append(piece)
        ordered = jnp.concatenate(pieces, 1)
        values = apply_rows(ordered, inv[l])
        field[l] = values
        r1p[l] = product(nt, values, vh[l, 5:7].reshape(128, part), vl[l, 5:7].reshape(128, part))
        if l % 2 == 1:
            pair = pl.ds(l - 1, 2)
            parts = [(r1p.at[pair], r1.at[z, pair], peer) for peer in z_peers]
            r1_steps.append(send(parts, r1.at[three, pair]))
    r1[z] = r1p[...]

    raw = None
    for l in range(leaves):
        block = product(nt, field[l], vh[l, 0:6].reshape(384, part), vl[l, 0:6].reshape(384, part))
        raw = block if raw is None else raw + block

    @pl.when(last_column)
    def _():
        core_wait(0, xc.at[three]).wait_recv()
        for copy in along_y_three:
            copy.start()
        cb[3:6] = xc[0:3]

    @pl.when(c == 1)
    def _():
        @pl.when(y < 3)
        def _():
            for copy in along_y_one:
                copy.start()
            cb[y] = core[3]

    rs_step.wait_recv()
    sum_a = rs[0] + rs[2] + rs[4] + rs[6]
    sum_b = rs[1] + rs[3] + rs[5] + rs[7]
    g3p[...] = low_low(sum_a[:, :, :128], sum_b[:, :, :128])
    g3[:, me] = g3p[...]
    ysp[...] = sum_a + sum_b
    ys[y] = ysp[...]
    g3_step = send([(g3p, g3.at[:, me], peer) for peer in zc_peers], g3.at[:, seven])
    ys_step = send([(ysp, ys.at[y], peer) for peer in y_peers], ys.at[three])
    g21_step.wait_recv()
    coupling = g21[0] + g21[1] + g21[2] + g21[3]
    zeros = jnp.zeros((64, 128), f32)
    coupling = jnp.concatenate(
        [jnp.concatenate([coupling[0], zeros], 1), jnp.concatenate([zeros, coupling[1]], 1)], 0
    )

    for step in r1_steps:
        step.wait_recv()
    s = [r1[0, l] + r1[1, l] + r1[2, l] + r1[3, l] for l in range(leaves)]
    s1 = [apply_rows(high_high(s[2 * n], s[2 * n + 1]), core[2 * n]) for n in range(2)]
    p2 = low_low(s[0] + s[1], s[2] + s[3]) - apply_rows(jnp.concatenate(s1, 1), coupling)
    s2 = apply_rows(p2, core[1])
    own = [
        low_low(s1[0], s2),
        jnp.where(low_lanes, turn(s1[0]), turn(s2)),
        jnp.where(low_lanes, s1[1], s2),
        high_high(s1[1], s2),
    ]
    r2p[...] = raw - product(nt, jnp.concatenate(own, 1), q1h[...], q1l[...])
    r2_step = send([(r2p, r2.at[me], peer) for peer in zc_peers], r2.at[seven])
    r2[me] = r2p[...]

    def correct(l, coefficients, levels):
        b_high, b_low = (t[l, levels[0]:levels[1]].reshape(-1, part) for t in (uh, ul))
        return product(nn, coefficients, b_high, b_low)

    for l in range(leaves):
        field[l] = field[l] - correct(l, own[l], (0, 2))

    @pl.when(c == 1)
    def _():
        @pl.when(y == 3)
        def _():
            core_wait(1, cb.at[three]).wait_recv()

        @pl.when(y < 3)
        def _():
            core_wait(1, cb.at[pl.ds(0, 5)]).wait_recv()

        to_sibling.start()

    ys_step.wait_recv()
    for n in range(2):
        g45p[4 * n : 4 * n + 4] = high_high(ys[2 * n, :, :, :128], ys[2 * n + 1, :, :, :128])
    halves = [ys[0, 2:4, :, 128:] + ys[1, 2:4, :, 128:], ys[2, 2:4, :, 128:] + ys[3, 2:4, :, 128:]]
    g45p[8:10] = low_low(halves[0], halves[1])
    xsp[...] = halves[0][1] + halves[1][1]
    g45[:, me] = g45p[...]
    xs[x] = xsp[...]
    xs_step = send([(xsp, xs.at[x], peer) for peer in x_peers], xs.at[three])
    g45_step = send([(g45p, g45.at[:, me], peer) for peer in zc_peers], g45.at[:, seven])

    g3_step.wait_recv()

    @pl.when(c == 1)
    def _():
        third.wait_recv()

    r2_step.wait_recv()
    p_a = r2[0] + r2[2] + r2[4] + r2[6]
    p_b = r2[1] + r2[3] + r2[5] + r2[7]
    s3 = apply_rows(low_low(p_a[:, 256:], p_b[:, 256:]), c3[...])
    r3p[...] = p_a[:, :256] + p_b[:, :256] - apply_rows(s3, g3[...].reshape(256, 128))
    r3_step = send([(r3p, r3.at[y], peer) for peer in y_peers], r3.at[three])
    r3[y] = r3p[...]

    xs_step.wait_recv()
    for n in range(2):
        g6p[n] = high_high(xs[2 * n], xs[2 * n + 1])
    g6[:, me] = g6p[...]
    g6_step = send([(g6p, g6.at[:, me], peer) for peer in zc_peers], g6.at[:, seven])

    @pl.when(c == 0)
    def _():
        to_sibling.wait_recv()

    g45_step.wait_recv()
    r3_step.wait_recv()
    s4, below = [], []
    for n in range(2):
        p4 = low_low(r3[2 * n, :, :128], r3[2 * n + 1, :, :128])
        s4.append(apply_rows(p4, cb[2 * n]))
        below.append(r3[2 * n] + r3[2 * n + 1] - apply_rows(s4[n], g45[4 * n : 4 * n + 4].reshape(256, 128)))
    s5 = apply_rows(high_high(below[0][:, :128], below[1][:, :128]), cb[1])
    r4p[...] = below[0][:, 128:] + below[1][:, 128:] - apply_rows(s5, g45[8:10].reshape(128, 128))
    r4_step = send([(r4p, r4.at[x], peer) for peer in x_peers], r4.at[three])
    r4[x] = r4p[...]

    own3 = jnp.where(c == 0, s3, turn(s3))
    own4 = jnp.where(y < 2, s4[0], s4[1])
    own4 = jnp.where(lax.rem(y, 2) == 1, own4, turn(own4))
    own5 = jnp.where(y < 2, s5, turn(s5))
    own34 = jnp.where(low_lanes, own3, own4)
    for l in range(leaves):
        field[l] = field[l] - correct(l, own34, (2, 4)) - correct(l, own5[:, :64], (4, 5))

    g6_step.wait_recv()
    coupling = jnp.concatenate(
        [
            jnp.concatenate([g6[0].reshape(64, 128), zeros], 1),
            jnp.concatenate([zeros, g6[1].reshape(64, 128)], 1),
        ],
        0,
    )
    r4_step.wait_recv()
    s6 = [apply_rows(low_low(r4[2 * n], r4[2 * n + 1]), cb[3 + 2 * n]) for n in range(2)]
    p7 = high_high(r4[0] + r4[1], r4[2] + r4[3]) - apply_rows(jnp.concatenate(s6, 1), coupling)
    s7 = apply_rows(p7, cb[4])
    own6 = jnp.where(x < 2, s6[0], s6[1])
    own6 = jnp.where(lax.rem(x, 2) == 0, own6, turn(own6))
    own7 = jnp.where(x < 2, turn(s7), s7)
    own67 = jnp.where(low_lanes, own6, own7)
    for l in range(leaves):
        out[l] = field[l] - correct(l, own67, (5, 7))

    for step in steps:
        step.wait_send()

    @pl.when(last_column)
    def _():
        core_wait(0, xc.at[three]).wait_send()
        core_wait(1, inv.at[0, pl.ds(0, 144)]).wait_send()

    @pl.when(c == 1)
    def _():
        to_sibling.wait_send()

        @pl.when(y < 3)
        def _():
            core_wait(1, cb.at[three]).wait_send()

    @pl.when(c == 0)
    def _():
        third.wait_send()


def per_device(*inputs):
    members, leaves, part = inputs[0].shape
    size = 4 * part
    vmem = pltpu.VMEM
    scratch = [
        vmem((4, leaves, members, part), f32),
        vmem((leaves, size), jnp.int32),
        vmem((leaves, part, size), f32),
        vmem((leaves, 7, 64, part), f32),
        vmem((leaves, 7, 64, part), f32),
        vmem((leaves, 128, 128), f32),
        vmem((leaves, 7, 64, part), bf16),
        vmem((leaves, 7, 64, part), bf16),
        vmem((leaves, 7, 64, part), bf16),
        vmem((leaves, 7, 64, part), bf16),
        vmem((384, 512), f32),
        vmem((384, 512), bf16),
        vmem((384, 512), bf16),
        vmem((4, 8, 8, 256), f32),
        vmem((2, 64, 128), f32),
        vmem((4, 2, 64, 128), f32),
        vmem((8, 4, 8, 256), f32),
        vmem((4, 8, 8, 128), f32),
        vmem((4, 4, 8, 256), f32),
        vmem((10, 8, 128), f32),
        vmem((10, 8, 8, 128), f32),
        vmem((4, 8, 128), f32),
        vmem((2, 8, 128), f32),
        vmem((2, 8, 8, 128), f32),
        vmem((4, 8, 128), f32),
        vmem((4, 8, 256), f32),
        vmem((8, 128), f32),
        vmem((4, 128, 128), f32),
        vmem((6, 128, 128), f32),
        vmem((128, 128), f32),
        vmem((leaves, members, part), f32),
        vmem((leaves, members, 128), f32),
        vmem((4, leaves, members, 128), f32),
        vmem((members, 384), f32),
        vmem((8, members, 384), f32),
        vmem((members, 256), f32),
        vmem((4, members, 256), f32),
        vmem((members, 128), f32),
        vmem((4, members, 128), f32),
        pltpu.SemaphoreType.DMA((6,)),
        pltpu.SemaphoreType.DMA((STEPS,)),
        pltpu.SemaphoreType.DMA((STEPS,)),
        pltpu.SemaphoreType.DMA((4,)),
        pltpu.SemaphoreType.DMA((4,)),
    ]
    result = pl.pallas_call(
        kernel,
        out_shape=jax.ShapeDtypeStruct((leaves, members, part), f32),
        in_specs=[pl.BlockSpec(memory_space=pl.ANY)] * 6,
        out_specs=pl.BlockSpec(memory_space=pltpu.VMEM),
        scratch_shapes=scratch,
        compiler_params=pltpu.CompilerParams(
            collective_id=0, has_side_effects=True, vmem_limit_bytes=53 * 2**20 + 832 * 2**10
        ),
    )(*inputs)
    return jnp.transpose(result, (1, 0, 2))


def solution(mesh):
    in_specs = (
        P(None, "leaf", "sub"),
        P("leaf", None),
        P("leaf", "sub", None),
        P(None, None, "leaf", "sub"),
        P(None, None, "leaf", "sub"),
        P("leaf", None, None),
    )
    return jax.shard_map(
        per_device, mesh=mesh, in_specs=in_specs, out_specs=P(None, "leaf", "sub"), check_vma=False
    )
```

```python
import math

import jax
import jax.numpy as jnp
from jax import lax
from jax.experimental import pallas as pl
from jax.experimental.pallas import tpu as pltpu
from jax.sharding import PartitionSpec as P

MESH = pl.DeviceIdType.MESH
f32, bf16 = jnp.float32, jnp.bfloat16

STEPS = 19


def split(value):
    high = value.astype(bf16)
    return high, (value - high.astype(f32)).astype(bf16)


def nt(a, b):
    return lax.dot_general(a, b, (((1,), (1,)), ((), ())), preferred_element_type=f32)


def nn(a, b):
    return lax.dot_general(a, b, (((1,), (0,)), ((), ())), preferred_element_type=f32)


def product(dot, a, b_high, b_low):
    rows = a.shape[0]
    a_high, a_low = split(a)
    both = dot(jnp.concatenate([a_high, a_low], 0), b_high)
    return both[:rows] + both[rows:] + dot(a_high, b_low)


def apply_rows(a, matrix):
    return product(nt, a, *split(matrix))


def kernel(
    right, order, inverse, left, column, cores,
    out,
    rhs, index, inv, u32, v32, core,
    uh, ul, vh, vl,
    fold_h, fold_l, low, q3a, q3b, g21p, g21, rsa, rsb, g3, ys, g45p, g45, xs, g6p, g6, g3p, ysp, xsp,
    xc, cb, c3,
    field, coefficients, r1p, r1, r2p, r2, r3p, r3, r4p, r4,
    load_sem, send_sem, recv_sem, c_send, c_recv,
):
    members, leaves, part = right.shape
    size = order.shape[1]
    leaf, z = lax.axis_index("leaf"), lax.axis_index("sub")
    c = lax.rem(leaf, 2)
    y = lax.rem(lax.div(leaf, 2), 4)
    x = lax.div(leaf, 8)
    me = 2 * z + c
    sibling = (leaf + 1 - 2 * c, z)
    z_peers = [(leaf, lax.rem(z + d, 4)) for d in (1, 2, 3)]
    zc_peers = [(leaf, lax.rem(z + d, 4)) for d in (1, 2, 3)]
    zc_peers += [(leaf + 1 - 2 * c, lax.rem(z + d, 4)) for d in (0, 1, 2, 3)]
    zc_index = [2 * lax.rem(z + d, 4) + c for d in (1, 2, 3)]
    zc_index += [2 * lax.rem(z + d, 4) + 1 - c for d in (0, 1, 2, 3)]
    y_peers = [(8 * x + 2 * lax.rem(y + d, 4) + c, z) for d in (1, 2, 3)]
    x_peers = [(8 * lax.rem(x + d, 4) + 2 * y + c, z) for d in (1, 2, 3)]

    steps = []

    def send(parts, landed):
        i = len(steps)
        for src, dst, device in parts:
            remote(send_sem.at[i], recv_sem.at[i], src, dst, device).start()
        steps.append(remote(send_sem.at[i], recv_sem.at[i], landed, landed, sibling))
        return steps[i]

    def remote(sent, received, src, dst, device):
        return pltpu.make_async_remote_copy(
            src_ref=src, dst_ref=dst, send_sem=sent, recv_sem=received,
            device_id=device, device_id_type=MESH,
        )

    loads = []

    def load(parts, landed):
        i = len(loads)
        for src, dst in parts:
            pltpu.make_async_copy(src, dst, load_sem.at[i]).start()
        loads.append(pltpu.make_async_copy(landed, landed, load_sem.at[i]))
        return loads[i]

    rhs_load = load([(right.at[:, l, :], rhs.at[z, l]) for l in range(leaves)], rhs.at[z])
    order_load = load([(order.at[pl.ds(l, 1)], index.at[l]) for l in range(leaves)], index)
    core_load = load([(cores, core)], core)
    slots = [(slice(3, 7), slice(0, 4)), (2, 4), (1, 5), (0, 6)]
    column_load = load(
        [(column.at[a, :, l, :], v32.at[l, b]) for l in range(leaves) for a, b in slots], v32
    )
    left_load = load([(left.at[:, :, l, :], u32.at[l]) for l in range(leaves)], u32)
    inverse_load = load([(inverse, inv)], inv)

    barrier = pltpu.get_barrier_semaphore()
    peers = zc_peers + y_peers + x_peers
    for peer in peers:
        pl.semaphore_signal(barrier, inc=1, device_id=peer, device_id_type=MESH)

    rhs_load.wait()
    pl.semaphore_wait(barrier, len(peers))
    three = pl.ds(0, 3)
    seven = pl.ds(0, 7)
    rhs_steps = [
        send([(rhs.at[z, l], rhs.at[z, l], peer) for peer in z_peers], rhs.at[three, l])
        for l in range(leaves)
    ]

    last_column = lax.rem(leaf, 8) == 7

    def core_copies(i, parts):
        return [remote(c_send.at[i], c_recv.at[i], *each) for each in parts]

    along_x = core_copies(0, [(core.at[3], xc.at[x], peer) for peer in x_peers])
    along_y_one = core_copies(1, [(core.at[3], cb.at[y], peer) for peer in y_peers])
    along_y_three = core_copies(1, [(xc.at[three], cb.at[pl.ds(3, 3)], peer) for peer in y_peers])
    to_sibling = remote(c_send.at[2], c_recv.at[2], cb, cb, sibling)
    third = remote(c_send.at[3], c_recv.at[3], core.at[3], c3, sibling)

    def core_wait(i, landed):
        return remote(c_send.at[i], c_recv.at[i], landed, landed, sibling)

    core_load.wait()

    @pl.when(last_column)
    def _():
        for copy in along_x:
            copy.start()
        xc[x] = core[3]

    @pl.when(c == 0)
    def _():
        third.start()
        c3[...] = core[3]

    low_lanes = lax.broadcasted_iota(jnp.int32, (1, 128), 1) < 64

    def norm(level):
        return 1.0 / math.sqrt(size * 2 ** (level - 1))

    def turn(a):
        return pltpu.roll(a, 64, a.ndim - 1)

    def low_low(a, b):
        return jnp.where(low_lanes, a, turn(b))

    def high_high(a, b):
        return jnp.where(low_lanes, turn(a), b)

    def each_leaf(body, unroll=False):
        lax.fori_loop(0, leaves, lambda l, none: body(l), None, unroll=unroll)

    def gram(l, slots, levels):
        a_high, a_low = split(v32[l, slots[0]:slots[1]].reshape(-1, part))
        b_high, b_low = split(u32[l, levels[0]:levels[1]].reshape(-1, part))
        return nt(a_high, b_high) + nt(a_low, b_high) + nt(a_high, b_low)

    column_load.wait()
    left_load.wait()
    for n in range(2):
        g21p[n] = low_low(*(gram(2 * n + j, (5, 6), (0, 2)) for j in range(2)))
    g21[z] = g21p[...]
    g21_step = send([(g21p, g21.at[z], peer) for peer in z_peers], g21.at[three])

    total = gram(0, (0, 4), (2, 6))
    for l in range(1, leaves):
        total += gram(l, (0, 4), (2, 6))
    q3a[...] = total[:128, :128].reshape(2, 8, 8, 128)
    q3b[...] = total[128:].reshape(2, 8, 8, 256)
    rsa[me] = q3a[:, me]
    rsb[me] = q3b[:, me]
    zc_pairs = list(zip(zc_index, zc_peers, strict=True))
    rsa_step = send([(q3a.at[:, i], rsa.at[me], peer) for i, peer in zc_pairs], rsa.at[seven])
    rsb_step = send([(q3b.at[:, i], rsb.at[me], peer) for i, peer in zc_pairs], rsb.at[seven])

    def split_bases(l):
        for k in range(7):
            vh[l, k], vl[l, k] = split(v32[l, k])
            uh[l, k], ul[l, k] = split(u32[l, k])

    each_leaf(split_bases, True)
    order_load.wait()
    inverse_load.wait()

    first = len(steps)
    for l in range(leaves):
        steps.append(remote(send_sem.at[first + l], recv_sem.at[first + l], r1.at[three, l], r1.at[three, l], sibling))
    r1_steps = steps[first:]

    def solve_leaf(l):
        remote(send_sem.at[l], recv_sem.at[l], rhs.at[three, l], rhs.at[three, l], sibling).wait_recv()
        pieces = []
        for u in range(8):
            place = index[l, :, 128 * u : 128 * u + 128]
            lane = jnp.broadcast_to(place & 127, (members, 128))
            tile = jnp.broadcast_to(place >> 7, (members, 128))
            piece = jnp.zeros((members, 128), f32)
            for t in range(8):
                source = rhs[t // 2, l, :, 128 * (t % 2) : 128 * (t % 2) + 128]
                piece = jnp.where(tile == t, jnp.take_along_axis(source, lane, axis=1), piece)
            pieces.append(piece)
        values = apply_rows(jnp.concatenate(pieces, 1), inv[l])
        field[l] = values
        r1p[l] = product(nt, values, vh[l, 5:7].reshape(128, part), vl[l, 5:7].reshape(128, part))
        for peer in z_peers:
            remote(send_sem.at[first + l], recv_sem.at[first + l], r1p.at[l], r1.at[z, l], peer).start()

    each_leaf(solve_leaf, True)
    r1[z] = r1p[...]

    def gram_low(l):
        low[:, pl.ds(pl.multiple_of(128 * l, 128), 128)] = gram(l, (0, 6), (0, 2))

    each_leaf(gram_low, True)

    def project(l, total):
        b_high, b_low = (t[l, 0:6].reshape(384, part) for t in (vh, vl))
        return total + product(nt, field[l], b_high, b_low)

    raw = lax.fori_loop(0, leaves, project, jnp.zeros((members, 384), f32), unroll=True)

    @pl.when(last_column)
    def _():
        core_wait(0, xc.at[three]).wait_recv()
        for copy in along_y_three:
            copy.start()
        cb[3:6] = xc[0:3]

    @pl.when(c == 1)
    def _():
        @pl.when(y < 3)
        def _():
            for copy in along_y_one:
                copy.start()
            cb[y] = core[3]

    rsa_step.wait_recv()
    rsb_step.wait_recv()
    sums = [[t[j] + t[2 + j] + t[4 + j] + t[6 + j] for j in range(2)] for t in (rsa, rsb)]
    for i in range(2):
        g3p[2 * i : 2 * i + 2] = low_low(sums[i][0][:, :, :128], sums[i][1][:, :, :128])
    ysp[0:2, :, :128] = sums[0][0] + sums[0][1]
    ysp[0:2, :, 128:] = jnp.zeros((2, 8, 128), f32)
    ysp[2:4] = sums[1][0] + sums[1][1]
    g3[:, me] = g3p[...]
    ys[y] = ysp[...]
    g3_step = send([(g3p, g3.at[:, me], peer) for peer in zc_peers], g3.at[:, seven])
    ys_step = send([(ysp, ys.at[y], peer) for peer in y_peers], ys.at[three])
    def fold_core(matrix, level, core_inverse):
        return norm(level) * product(nn, matrix, *split(core_inverse))

    quarter = [low[:, 128 * l : 128 * l + 128] for l in range(leaves)]
    for n in range(2):
        lanes = slice(128 * n, 128 * n + 128)
        first_half = low_low(quarter[2 * n], quarter[2 * n + 1])
        fold_h[:, lanes], fold_l[:, lanes] = split(fold_core(first_half, 1, core[2 * n]))
    second = fold_core(high_high(quarter[0] + quarter[1], quarter[2] + quarter[3]), 2, core[1])
    fold_h[:, 256:], fold_l[:, 256:] = split(second)
    g21_step.wait_recv()
    coupling = g21[0] + g21[1] + g21[2] + g21[3]
    zeros = jnp.zeros((64, 128), f32)
    coupling = jnp.concatenate(
        [jnp.concatenate([coupling[0], zeros], 1), jnp.concatenate([zeros, coupling[1]], 1)], 0
    )

    fold21 = split(
        jnp.concatenate([fold_core(coupling[:, 128 * n : 128 * n + 128], 1, core[2 * n]) for n in range(2)], 1)
    )

    for step in r1_steps:
        step.wait_recv()
    s = [r1[0, l] + r1[1, l] + r1[2, l] + r1[3, l] for l in range(leaves)]
    p1 = [high_high(s[2 * n], s[2 * n + 1]) for n in range(2)]
    p2 = low_low(s[0] + s[1], s[2] + s[3])
    p2 -= product(nt, jnp.concatenate(p1, 1), *fold21)
    r2p[...] = raw - product(nt, jnp.concatenate([*p1, p2], 1), fold_h[...], fold_l[...])
    r2_step = send([(r2p, r2.at[me], peer) for peer in zc_peers], r2.at[seven])
    r2[me] = r2p[...]

    s1 = [apply_rows(norm(1) * p1[n], core[2 * n]) for n in range(2)]
    s2 = apply_rows(norm(2) * p2, core[1])
    own = [
        low_low(s1[0], s2),
        jnp.where(low_lanes, turn(s1[0]), turn(s2)),
        jnp.where(low_lanes, s1[1], s2),
        high_high(s1[1], s2),
    ]

    def correct(l, coefficients, levels):
        b_high, b_low = (t[l, levels[0]:levels[1]].reshape(-1, part) for t in (uh, ul))
        return product(nn, coefficients, b_high, b_low)

    for l in range(leaves):
        coefficients[l] = own[l]

    def correct_low(l):
        field[l] = field[l] - correct(l, coefficients[l], (0, 2))

    each_leaf(correct_low, True)

    @pl.when(c == 1)
    def _():
        @pl.when(y == 3)
        def _():
            core_wait(1, cb.at[three]).wait_recv()

        @pl.when(y < 3)
        def _():
            core_wait(1, cb.at[pl.ds(0, 5)]).wait_recv()

        to_sibling.start()

    ys_step.wait_recv()
    for n in range(2):
        g45p[3 * n : 3 * n + 3] = high_high(ys[2 * n, 1:4, :, :128], ys[2 * n + 1, 1:4, :, :128])
    halves = [ys[0, 2:4, :, 128:] + ys[1, 2:4, :, 128:], ys[2, 2:4, :, 128:] + ys[3, 2:4, :, 128:]]
    g45p[6:8] = low_low(halves[0], halves[1])
    xsp[...] = halves[0][1] + halves[1][1]
    g45[:, me] = g45p[...]
    xs[x] = xsp[...]
    xs_step = send([(xsp, xs.at[x], peer) for peer in x_peers], xs.at[three])
    g45_step = send([(g45p, g45.at[:, me], peer) for peer in zc_peers], g45.at[:, seven])

    g3_step.wait_recv()

    @pl.when(c == 1)
    def _():
        third.wait_recv()

    fold3 = split(fold_core(g3[...].reshape(256, 128), 3, c3[...]))
    r2_step.wait_recv()
    p_a = r2[0] + r2[2] + r2[4] + r2[6]
    p_b = r2[1] + r2[3] + r2[5] + r2[7]
    p3 = low_low(p_a[:, 256:], p_b[:, 256:])
    r3p[...] = p_a[:, :256] + p_b[:, :256] - product(nt, p3, *fold3)
    r3_step = send([(r3p, r3.at[y], peer) for peer in y_peers], r3.at[three])
    r3[y] = r3p[...]

    xs_step.wait_recv()
    for n in range(2):
        g6p[n] = high_high(xs[2 * n], xs[2 * n + 1])
    g6[:, me] = g6p[...]
    g6_step = send([(g6p, g6.at[:, me], peer) for peer in zc_peers], g6.at[:, seven])

    @pl.when(c == 0)
    def _():
        to_sibling.wait_recv()

    g45_step.wait_recv()
    fold5 = fold_core(g45[6:8].reshape(128, 128), 5, cb[1])
    fold45 = []
    for n in range(2):
        fold4 = fold_core(g45[3 * n : 3 * n + 3].reshape(192, 128), 4, cb[2 * n])
        half = fold5[:, 64 * n : 64 * n + 64]
        fold45.append(fold4[64:] - product(nn, half, *split(fold4[:64])))
    fold45 = split(jnp.concatenate([*fold45, fold5], 1))
    r3_step.wait_recv()
    p4 = [low_low(r3[2 * n, :, :128], r3[2 * n + 1, :, :128]) for n in range(2)]
    pair = [r3[2 * n] + r3[2 * n + 1] for n in range(2)]
    p5 = high_high(pair[0][:, :128], pair[1][:, :128])
    r4p[...] = (
        pair[0][:, 128:] + pair[1][:, 128:] - product(nt, jnp.concatenate([*p4, p5], 1), *fold45)
    )
    r4_step = send([(r4p, r4.at[x], peer) for peer in x_peers], r4.at[three])
    r4[x] = r4p[...]

    s3 = apply_rows(norm(3) * p3, c3[...])
    s4 = [apply_rows(norm(4) * p4[n], cb[2 * n]) for n in range(2)]
    below = [apply_rows(s4[n], g45[3 * n].reshape(64, 128)) for n in range(2)]
    s5 = apply_rows(norm(5) * (p5 - jnp.concatenate(below, 1)), cb[1])
    own3 = jnp.where(c == 0, s3, turn(s3))
    own4 = jnp.where(y < 2, s4[0], s4[1])
    own4 = jnp.where(lax.rem(y, 2) == 1, own4, turn(own4))
    own5 = jnp.where(y < 2, s5, turn(s5))
    own34 = jnp.where(low_lanes, own3, own4)

    def correct_middle(l):
        field[l] = field[l] - correct(l, own34, (2, 4)) - correct(l, own5[:, :64], (4, 5))

    each_leaf(correct_middle, True)

    g6_step.wait_recv()
    coupling = jnp.concatenate(
        [
            jnp.concatenate([g6[0].reshape(64, 128), zeros], 1),
            jnp.concatenate([zeros, g6[1].reshape(64, 128)], 1),
        ],
        0,
    )
    c7 = norm(7) * jnp.where(x < 2, cb[4, :64], cb[4, 64:])
    c6 = jnp.where(x < 2, cb[3], cb[5])
    c6 = norm(6) * jnp.where(lax.rem(x, 2) == 0, c6[:64], c6[64:])
    fold67 = []
    for n in range(2):
        lanes = slice(128 * n, 128 * n + 128)
        below7 = fold_core(product(nn, c7, *split(coupling[:, lanes])), 6, cb[3 + 2 * n])
        here = jnp.where(lax.div(x, 2) == n, c6, zeros)
        fold67.append(jnp.concatenate([here, -below7], 0))
    fold67.append(jnp.concatenate([zeros, c7], 0))
    fold67 = split(jnp.concatenate(fold67, 1))
    r4_step.wait_recv()
    p6 = [low_low(r4[2 * n], r4[2 * n + 1]) for n in range(2)]
    p7 = high_high(r4[0] + r4[1], r4[2] + r4[3])
    own67 = product(nt, jnp.concatenate([*p6, p7], 1), *fold67)

    def correct_high(l):
        out[l] = field[l] - correct(l, own67, (5, 7))

    each_leaf(correct_high, True)

    for step in steps:
        step.wait_send()

    @pl.when(last_column)
    def _():
        core_wait(0, xc.at[three]).wait_send()
        core_wait(1, inv.at[0, pl.ds(0, 144)]).wait_send()

    @pl.when(c == 1)
    def _():
        to_sibling.wait_send()

        @pl.when(y < 3)
        def _():
            core_wait(1, cb.at[three]).wait_send()

    @pl.when(c == 0)
    def _():
        third.wait_send()


def per_device(*inputs):
    members, leaves, part = inputs[0].shape
    size = 4 * part
    vmem = pltpu.VMEM
    scratch = [
        vmem((4, leaves, members, part), f32),
        vmem((leaves, 1, size), jnp.int32),
        vmem((leaves, part, size), f32),
        vmem((leaves, 7, 64, part), f32),
        vmem((leaves, 7, 64, part), f32),
        vmem((leaves, 128, 128), f32),
        vmem((leaves, 7, 64, part), bf16),
        vmem((leaves, 7, 64, part), bf16),
        vmem((leaves, 7, 64, part), bf16),
        vmem((leaves, 7, 64, part), bf16),
        vmem((384, 384), bf16),
        vmem((384, 384), bf16),
        vmem((384, 512), f32),
        vmem((2, 8, 8, 128), f32),
        vmem((2, 8, 8, 256), f32),
        vmem((2, 64, 128), f32),
        vmem((4, 2, 64, 128), f32),
        vmem((8, 2, 8, 128), f32),
        vmem((8, 2, 8, 256), f32),
        vmem((4, 8, 8, 128), f32),
        vmem((4, 4, 8, 256), f32),
        vmem((8, 8, 128), f32),
        vmem((8, 8, 8, 128), f32),
        vmem((4, 8, 128), f32),
        vmem((2, 8, 128), f32),
        vmem((2, 8, 8, 128), f32),
        vmem((4, 8, 128), f32),
        vmem((4, 8, 256), f32),
        vmem((8, 128), f32),
        vmem((4, 128, 128), f32),
        vmem((6, 128, 128), f32),
        vmem((128, 128), f32),
        vmem((leaves, members, part), f32),
        vmem((leaves, members, 128), f32),
        vmem((leaves, members, 128), f32),
        vmem((4, leaves, members, 128), f32),
        vmem((members, 384), f32),
        vmem((8, members, 384), f32),
        vmem((members, 256), f32),
        vmem((4, members, 256), f32),
        vmem((members, 128), f32),
        vmem((4, members, 128), f32),
        pltpu.SemaphoreType.DMA((6,)),
        pltpu.SemaphoreType.DMA((STEPS,)),
        pltpu.SemaphoreType.DMA((STEPS,)),
        pltpu.SemaphoreType.DMA((4,)),
        pltpu.SemaphoreType.DMA((4,)),
    ]
    result = pl.pallas_call(
        kernel,
        out_shape=jax.ShapeDtypeStruct((leaves, members, part), f32),
        in_specs=[pl.BlockSpec(memory_space=pl.ANY)] * 6,
        out_specs=pl.BlockSpec(memory_space=pltpu.VMEM),
        scratch_shapes=scratch,
        compiler_params=pltpu.CompilerParams(
            collective_id=0, has_side_effects=True, vmem_limit_bytes=53 * 2**20 + 832 * 2**10
        ),
    )(*inputs)
    return jnp.transpose(result, (1, 0, 2))


def solution(mesh):
    in_specs = (
        P(None, "leaf", "sub"),
        P("leaf", None),
        P("leaf", "sub", None),
        P(None, None, "leaf", "sub"),
        P(None, None, "leaf", "sub"),
        P("leaf", None, None),
    )
    return jax.shard_map(
        per_device, mesh=mesh, in_specs=in_specs, out_specs=P(None, "leaf", "sub"), check_vma=False
    )
```

```python
import math

import jax
import jax.numpy as jnp
from jax import lax
from jax.experimental import pallas as pl
from jax.experimental.pallas import tpu as pltpu
from jax.sharding import PartitionSpec as P

MESH = pl.DeviceIdType.MESH
f32, bf16 = jnp.float32, jnp.bfloat16

STEPS = 19


def split(value):
    high = value.astype(bf16)
    return high, (value - high.astype(f32)).astype(bf16)


def nt(a, b):
    return lax.dot_general(a, b, (((1,), (1,)), ((), ())), preferred_element_type=f32)


def nn(a, b):
    return lax.dot_general(a, b, (((1,), (0,)), ((), ())), preferred_element_type=f32)


def product(dot, a, b_high, b_low):
    rows = a.shape[0]
    a_high, a_low = split(a)
    both = dot(jnp.concatenate([a_high, a_low], 0), b_high)
    return both[:rows] + both[rows:] + dot(a_high, b_low)


def apply_rows(a, matrix):
    return product(nt, a, *split(matrix))


def kernel(
    right, order, inverse, left, column, cores,
    out,
    rhs, index, inv, u32, v32, core,
    uh, ul, vh, vl,
    fold_h, fold_l, low, q3a, q3b, g21p, g21, rsa, rsb, g3, ys, g45p, g45, xs, g6p, g6, g3p, ysp, xsp,
    xc, cb, c3,
    field, coefficients, r1p, r1, r2p, r2, r3p, r3, r4p, r4,
    load_sem, send_sem, recv_sem, c_send, c_recv,
):
    members, leaves, part = right.shape
    size = order.shape[1]
    leaf, z = lax.axis_index("leaf"), lax.axis_index("sub")
    c = lax.rem(leaf, 2)
    y = lax.rem(lax.div(leaf, 2), 4)
    x = lax.div(leaf, 8)
    me = 2 * z + c
    sibling = (leaf + 1 - 2 * c, z)
    z_peers = [(leaf, lax.rem(z + d, 4)) for d in (1, 2, 3)]
    zc_peers = [(leaf, lax.rem(z + d, 4)) for d in (1, 2, 3)]
    zc_peers += [(leaf + 1 - 2 * c, lax.rem(z + d, 4)) for d in (0, 1, 2, 3)]
    zc_index = [2 * lax.rem(z + d, 4) + c for d in (1, 2, 3)]
    zc_index += [2 * lax.rem(z + d, 4) + 1 - c for d in (0, 1, 2, 3)]
    y_peers = [(8 * x + 2 * lax.rem(y + d, 4) + c, z) for d in (1, 2, 3)]
    x_peers = [(8 * lax.rem(x + d, 4) + 2 * y + c, z) for d in (1, 2, 3)]

    steps = []

    def send(parts, landed):
        i = len(steps)
        for src, dst, device in parts:
            remote(send_sem.at[i], recv_sem.at[i], src, dst, device).start()
        steps.append(remote(send_sem.at[i], recv_sem.at[i], landed, landed, sibling))
        return steps[i]

    def remote(sent, received, src, dst, device):
        return pltpu.make_async_remote_copy(
            src_ref=src, dst_ref=dst, send_sem=sent, recv_sem=received,
            device_id=device, device_id_type=MESH,
        )

    loads = []

    def load(parts, landed):
        i = len(loads)
        for src, dst in parts:
            pltpu.make_async_copy(src, dst, load_sem.at[i]).start()
        loads.append(pltpu.make_async_copy(landed, landed, load_sem.at[i]))
        return loads[i]

    rhs_load = load([(right.at[:, l, :], rhs.at[z, l]) for l in range(leaves)], rhs.at[z])
    order_load = load([(order.at[pl.ds(l, 1)], index.at[l]) for l in range(leaves)], index)
    core_load = load([(cores, core)], core)
    slots = [(slice(3, 7), slice(0, 4)), (2, 4), (1, 5), (0, 6)]
    column_load = load(
        [(column.at[a, :, l, :], v32.at[l, b]) for l in range(leaves) for a, b in slots], v32
    )
    left_load = load([(left.at[:, :, l, :], u32.at[l]) for l in range(leaves)], u32)
    inverse_load = load([(inverse, inv)], inv)

    barrier = pltpu.get_barrier_semaphore()
    peers = zc_peers + y_peers + x_peers
    for peer in peers:
        pl.semaphore_signal(barrier, inc=1, device_id=peer, device_id_type=MESH)

    rhs_load.wait()
    pl.semaphore_wait(barrier, len(peers))
    three = pl.ds(0, 3)
    seven = pl.ds(0, 7)
    rhs_steps = [
        send([(rhs.at[z, l], rhs.at[z, l], peer) for peer in z_peers], rhs.at[three, l])
        for l in range(leaves)
    ]

    last_column = lax.rem(leaf, 8) == 7

    def core_copies(i, parts):
        return [remote(c_send.at[i], c_recv.at[i], *each) for each in parts]

    along_x = core_copies(0, [(core.at[3], xc.at[x], peer) for peer in x_peers])
    along_y_one = core_copies(1, [(core.at[3], cb.at[y], peer) for peer in y_peers])
    along_y_three = core_copies(1, [(xc.at[three], cb.at[pl.ds(3, 3)], peer) for peer in y_peers])
    to_sibling = remote(c_send.at[2], c_recv.at[2], cb, cb, sibling)
    third = remote(c_send.at[3], c_recv.at[3], core.at[3], c3, sibling)

    def core_wait(i, landed):
        return remote(c_send.at[i], c_recv.at[i], landed, landed, sibling)

    core_load.wait()

    @pl.when(last_column)
    def _():
        for copy in along_x:
            copy.start()
        xc[x] = core[3]

    @pl.when(c == 0)
    def _():
        third.start()
        c3[...] = core[3]

    low_lanes = lax.broadcasted_iota(jnp.int32, (1, 128), 1) < 64

    def norm(level):
        return 1.0 / math.sqrt(size * 2 ** (level - 1))

    def turn(a):
        return pltpu.roll(a, 64, a.ndim - 1)

    def low_low(a, b):
        return jnp.where(low_lanes, a, turn(b))

    def high_high(a, b):
        return jnp.where(low_lanes, turn(a), b)

    def each_leaf(body, unroll=False):
        lax.fori_loop(0, leaves, lambda l, none: body(l), None, unroll=unroll)

    def gram(l, slots, levels):
        a_high, a_low = split(v32[l, slots[0]:slots[1]].reshape(-1, part))
        b_high, b_low = split(u32[l, levels[0]:levels[1]].reshape(-1, part))
        return nt(a_high, b_high) + nt(a_low, b_high) + nt(a_high, b_low)

    column_load.wait()
    left_load.wait()
    for n in range(2):
        g21p[n] = low_low(*(gram(2 * n + j, (5, 6), (0, 2)) for j in range(2)))
    g21[z] = g21p[...]
    g21_step = send([(g21p, g21.at[z], peer) for peer in z_peers], g21.at[three])

    total = gram(0, (0, 4), (2, 6))
    for l in range(1, leaves):
        total += gram(l, (0, 4), (2, 6))
    q3a[...] = total[:128, :128].reshape(2, 8, 8, 128)
    q3b[...] = total[128:].reshape(2, 8, 8, 256)
    rsa[me] = q3a[:, me]
    rsb[me] = q3b[:, me]
    for step in rhs_steps:
        step.wait_send()
    zc_pairs = list(zip(zc_index, zc_peers, strict=True))
    rsa_step = send([(q3a.at[:, i], rsa.at[me], peer) for i, peer in zc_pairs], rsa.at[seven])
    rsb_step = send([(q3b.at[:, i], rsb.at[me], peer) for i, peer in zc_pairs], rsb.at[seven])

    def split_bases(l):
        for k in range(7):
            vh[l, k], vl[l, k] = split(v32[l, k])
            uh[l, k], ul[l, k] = split(u32[l, k])

    each_leaf(split_bases, True)
    order_load.wait()
    inverse_load.wait()

    first = len(steps)
    for l in range(leaves):
        steps.append(remote(send_sem.at[first + l], recv_sem.at[first + l], r1.at[three, l], r1.at[three, l], sibling))
    r1_steps = steps[first:]

    def solve_leaf(l):
        remote(send_sem.at[l], recv_sem.at[l], rhs.at[three, l], rhs.at[three, l], sibling).wait_recv()
        pieces = []
        for u in range(8):
            place = index[l, :, 128 * u : 128 * u + 128]
            lane = jnp.broadcast_to(place & 127, (members, 128))
            tile = jnp.broadcast_to(place >> 7, (members, 128))
            piece = jnp.zeros((members, 128), f32)
            for t in range(8):
                source = rhs[t // 2, l, :, 128 * (t % 2) : 128 * (t % 2) + 128]
                piece = jnp.where(tile == t, jnp.take_along_axis(source, lane, axis=1), piece)
            pieces.append(piece)
        values = apply_rows(jnp.concatenate(pieces, 1), inv[l])
        field[l] = values
        r1p[l] = product(nt, values, vh[l, 5:7].reshape(128, part), vl[l, 5:7].reshape(128, part))
        for peer in z_peers:
            remote(send_sem.at[first + l], recv_sem.at[first + l], r1p.at[l], r1.at[z, l], peer).start()

    each_leaf(solve_leaf, True)
    r1[z] = r1p[...]

    def gram_low(l):
        low[:, pl.ds(pl.multiple_of(128 * l, 128), 128)] = gram(l, (0, 6), (0, 2))

    each_leaf(gram_low, True)

    def project(l, total):
        b_high, b_low = (t[l, 0:6].reshape(384, part) for t in (vh, vl))
        return total + product(nt, field[l], b_high, b_low)

    raw = lax.fori_loop(0, leaves, project, jnp.zeros((members, 384), f32), unroll=True)

    @pl.when(last_column)
    def _():
        core_wait(0, xc.at[three]).wait_recv()
        for copy in along_y_three:
            copy.start()
        cb[3:6] = xc[0:3]

    @pl.when(c == 1)
    def _():
        @pl.when(y < 3)
        def _():
            for copy in along_y_one:
                copy.start()
            cb[y] = core[3]

    rsa_step.wait_recv()
    rsb_step.wait_recv()
    sums = [[t[j] + t[2 + j] + t[4 + j] + t[6 + j] for j in range(2)] for t in (rsa, rsb)]
    for i in range(2):
        g3p[2 * i : 2 * i + 2] = low_low(sums[i][0][:, :, :128], sums[i][1][:, :, :128])
    ysp[0:2, :, :128] = sums[0][0] + sums[0][1]
    ysp[0:2, :, 128:] = jnp.zeros((2, 8, 128), f32)
    ysp[2:4] = sums[1][0] + sums[1][1]
    g3[:, me] = g3p[...]
    ys[y] = ysp[...]
    g3_step = send([(g3p, g3.at[:, me], peer) for peer in zc_peers], g3.at[:, seven])
    ys_step = send([(ysp, ys.at[y], peer) for peer in y_peers], ys.at[three])
    def fold_core(matrix, level, core_inverse):
        return norm(level) * product(nn, matrix, *split(core_inverse))

    quarter = [low[:, 128 * l : 128 * l + 128] for l in range(leaves)]
    for n in range(2):
        lanes = slice(128 * n, 128 * n + 128)
        first_half = low_low(quarter[2 * n], quarter[2 * n + 1])
        fold_h[:, lanes], fold_l[:, lanes] = split(fold_core(first_half, 1, core[2 * n]))
    second = fold_core(high_high(quarter[0] + quarter[1], quarter[2] + quarter[3]), 2, core[1])
    fold_h[:, 256:], fold_l[:, 256:] = split(second)
    g21_step.wait_recv()
    coupling = g21[0] + g21[1] + g21[2] + g21[3]
    zeros = jnp.zeros((64, 128), f32)
    coupling = jnp.concatenate(
        [jnp.concatenate([coupling[0], zeros], 1), jnp.concatenate([zeros, coupling[1]], 1)], 0
    )

    fold21 = split(
        jnp.concatenate([fold_core(coupling[:, 128 * n : 128 * n + 128], 1, core[2 * n]) for n in range(2)], 1)
    )

    for step in r1_steps:
        step.wait_recv()
    s = [r1[0, l] + r1[1, l] + r1[2, l] + r1[3, l] for l in range(leaves)]
    p1 = [high_high(s[2 * n], s[2 * n + 1]) for n in range(2)]
    p2 = low_low(s[0] + s[1], s[2] + s[3])
    p2 -= product(nt, jnp.concatenate(p1, 1), *fold21)
    r2p[...] = raw - product(nt, jnp.concatenate([*p1, p2], 1), fold_h[...], fold_l[...])
    r2_step = send([(r2p, r2.at[me], peer) for peer in zc_peers], r2.at[seven])
    r2[me] = r2p[...]

    ys_step.wait_recv()
    for n in range(2):
        g45p[3 * n : 3 * n + 3] = high_high(ys[2 * n, 1:4, :, :128], ys[2 * n + 1, 1:4, :, :128])
    halves = [ys[0, 2:4, :, 128:] + ys[1, 2:4, :, 128:], ys[2, 2:4, :, 128:] + ys[3, 2:4, :, 128:]]
    g45p[6:8] = low_low(halves[0], halves[1])
    xsp[...] = halves[0][1] + halves[1][1]
    g45[:, me] = g45p[...]
    xs[x] = xsp[...]
    xs_step = send([(xsp, xs.at[x], peer) for peer in x_peers], xs.at[three])
    g45_step = send([(g45p, g45.at[:, me], peer) for peer in zc_peers], g45.at[:, seven])

    s1 = [apply_rows(norm(1) * p1[n], core[2 * n]) for n in range(2)]
    s2 = apply_rows(norm(2) * p2, core[1])
    own = [
        low_low(s1[0], s2),
        jnp.where(low_lanes, turn(s1[0]), turn(s2)),
        jnp.where(low_lanes, s1[1], s2),
        high_high(s1[1], s2),
    ]

    def correct(l, coefficients, levels):
        b_high, b_low = (t[l, levels[0]:levels[1]].reshape(-1, part) for t in (uh, ul))
        return product(nn, coefficients, b_high, b_low)

    for l in range(leaves):
        coefficients[l] = own[l]

    def correct_low(l):
        field[l] = field[l] - correct(l, coefficients[l], (0, 2))

    each_leaf(correct_low, True)

    @pl.when(c == 1)
    def _():
        @pl.when(y == 3)
        def _():
            core_wait(1, cb.at[three]).wait_recv()

        @pl.when(y < 3)
        def _():
            core_wait(1, cb.at[pl.ds(0, 5)]).wait_recv()

        to_sibling.start()

    g3_step.wait_recv()

    @pl.when(c == 1)
    def _():
        third.wait_recv()

    fold3 = split(fold_core(g3[...].reshape(256, 128), 3, c3[...]))
    r2_step.wait_recv()
    p_a = r2[0] + r2[2] + r2[4] + r2[6]
    p_b = r2[1] + r2[3] + r2[5] + r2[7]
    p3 = low_low(p_a[:, 256:], p_b[:, 256:])
    r3p[...] = p_a[:, :256] + p_b[:, :256] - product(nt, p3, *fold3)
    r3_step = send([(r3p, r3.at[y], peer) for peer in y_peers], r3.at[three])
    r3[y] = r3p[...]

    xs_step.wait_recv()
    for n in range(2):
        g6p[n] = high_high(xs[2 * n], xs[2 * n + 1])
    g6[:, me] = g6p[...]
    g6_step = send([(g6p, g6.at[:, me], peer) for peer in zc_peers], g6.at[:, seven])

    @pl.when(c == 0)
    def _():
        to_sibling.wait_recv()

    g45_step.wait_recv()
    fold5 = fold_core(g45[6:8].reshape(128, 128), 5, cb[1])
    fold45 = []
    for n in range(2):
        fold4 = fold_core(g45[3 * n : 3 * n + 3].reshape(192, 128), 4, cb[2 * n])
        half = fold5[:, 64 * n : 64 * n + 64]
        fold45.append(fold4[64:] - product(nn, half, *split(fold4[:64])))
    fold45 = split(jnp.concatenate([*fold45, fold5], 1))
    r3_step.wait_recv()
    p4 = [low_low(r3[2 * n, :, :128], r3[2 * n + 1, :, :128]) for n in range(2)]
    pair = [r3[2 * n] + r3[2 * n + 1] for n in range(2)]
    p5 = high_high(pair[0][:, :128], pair[1][:, :128])
    r4p[...] = (
        pair[0][:, 128:] + pair[1][:, 128:] - product(nt, jnp.concatenate([*p4, p5], 1), *fold45)
    )
    r4_step = send([(r4p, r4.at[x], peer) for peer in x_peers], r4.at[three])
    r4[x] = r4p[...]

    s3 = apply_rows(norm(3) * p3, c3[...])
    s4 = [apply_rows(norm(4) * p4[n], cb[2 * n]) for n in range(2)]
    below = [apply_rows(s4[n], g45[3 * n].reshape(64, 128)) for n in range(2)]
    s5 = apply_rows(norm(5) * (p5 - jnp.concatenate(below, 1)), cb[1])
    own3 = jnp.where(c == 0, s3, turn(s3))
    own4 = jnp.where(y < 2, s4[0], s4[1])
    own4 = jnp.where(lax.rem(y, 2) == 1, own4, turn(own4))
    own5 = jnp.where(y < 2, s5, turn(s5))
    own34 = jnp.where(low_lanes, own3, own4)

    def correct_middle(l):
        field[l] = field[l] - correct(l, own34, (2, 4)) - correct(l, own5[:, :64], (4, 5))

    each_leaf(correct_middle, True)

    g6_step.wait_recv()
    coupling = jnp.concatenate(
        [
            jnp.concatenate([g6[0].reshape(64, 128), zeros], 1),
            jnp.concatenate([zeros, g6[1].reshape(64, 128)], 1),
        ],
        0,
    )
    c7 = norm(7) * jnp.where(x < 2, cb[4, :64], cb[4, 64:])
    c6 = jnp.where(x < 2, cb[3], cb[5])
    c6 = norm(6) * jnp.where(lax.rem(x, 2) == 0, c6[:64], c6[64:])
    fold67 = []
    for n in range(2):
        lanes = slice(128 * n, 128 * n + 128)
        below7 = fold_core(product(nn, c7, *split(coupling[:, lanes])), 6, cb[3 + 2 * n])
        here = jnp.where(lax.div(x, 2) == n, c6, zeros)
        fold67.append(jnp.concatenate([here, -below7], 0))
    fold67.append(jnp.concatenate([zeros, c7], 0))
    fold67 = split(jnp.concatenate(fold67, 1))
    r4_step.wait_recv()
    p6 = [low_low(r4[2 * n], r4[2 * n + 1]) for n in range(2)]
    p7 = high_high(r4[0] + r4[1], r4[2] + r4[3])
    own67 = product(nt, jnp.concatenate([*p6, p7], 1), *fold67)

    def correct_high(l):
        out[l] = field[l] - correct(l, own67, (5, 7))

    each_leaf(correct_high, True)

    for step in steps[leaves:]:
        step.wait_send()

    @pl.when(last_column)
    def _():
        core_wait(0, xc.at[three]).wait_send()
        core_wait(1, inv.at[0, pl.ds(0, 144)]).wait_send()

    @pl.when(c == 1)
    def _():
        to_sibling.wait_send()

        @pl.when(y < 3)
        def _():
            core_wait(1, cb.at[three]).wait_send()

    @pl.when(c == 0)
    def _():
        third.wait_send()


def per_device(*inputs):
    members, leaves, part = inputs[0].shape
    size = 4 * part
    vmem = pltpu.VMEM
    scratch = [
        vmem((4, leaves, members, part), f32),
        vmem((leaves, 1, size), jnp.int32),
        vmem((leaves, part, size), f32),
        vmem((leaves, 7, 64, part), f32),
        vmem((leaves, 7, 64, part), f32),
        vmem((leaves, 128, 128), f32),
        vmem((leaves, 7, 64, part), bf16),
        vmem((leaves, 7, 64, part), bf16),
        vmem((leaves, 7, 64, part), bf16),
        vmem((leaves, 7, 64, part), bf16),
        vmem((384, 384), bf16),
        vmem((384, 384), bf16),
        vmem((384, 512), f32),
        vmem((2, 8, 8, 128), f32),
        vmem((2, 8, 8, 256), f32),
        vmem((2, 64, 128), f32),
        vmem((4, 2, 64, 128), f32),
        vmem((8, 2, 8, 128), f32),
        vmem((8, 2, 8, 256), f32),
        vmem((4, 8, 8, 128), f32),
        vmem((4, 4, 8, 256), f32),
        vmem((8, 8, 128), f32),
        vmem((8, 8, 8, 128), f32),
        vmem((4, 8, 128), f32),
        vmem((2, 8, 128), f32),
        vmem((2, 8, 8, 128), f32),
        vmem((4, 8, 128), f32),
        vmem((4, 8, 256), f32),
        vmem((8, 128), f32),
        vmem((4, 128, 128), f32),
        vmem((6, 128, 128), f32),
        vmem((128, 128), f32),
        vmem((leaves, members, part), f32),
        vmem((leaves, members, 128), f32),
        vmem((leaves, members, 128), f32),
        vmem((4, leaves, members, 128), f32),
        vmem((members, 384), f32),
        vmem((8, members, 384), f32),
        vmem((members, 256), f32),
        vmem((4, members, 256), f32),
        vmem((members, 128), f32),
        vmem((4, members, 128), f32),
        pltpu.SemaphoreType.DMA((6,)),
        pltpu.SemaphoreType.DMA((STEPS,)),
        pltpu.SemaphoreType.DMA((STEPS,)),
        pltpu.SemaphoreType.DMA((4,)),
        pltpu.SemaphoreType.DMA((4,)),
    ]
    result = pl.pallas_call(
        kernel,
        out_shape=jax.ShapeDtypeStruct((leaves, members, part), f32),
        in_specs=[pl.BlockSpec(memory_space=pl.ANY)] * 6,
        out_specs=pl.BlockSpec(memory_space=pltpu.VMEM),
        scratch_shapes=scratch,
        compiler_params=pltpu.CompilerParams(
            collective_id=0, has_side_effects=True, vmem_limit_bytes=53 * 2**20 + 832 * 2**10
        ),
    )(*inputs)
    return jnp.transpose(result, (1, 0, 2))


def solution(mesh):
    in_specs = (
        P(None, "leaf", "sub"),
        P("leaf", None),
        P("leaf", "sub", None),
        P(None, None, "leaf", "sub"),
        P(None, None, "leaf", "sub"),
        P("leaf", None, None),
    )
    return jax.shard_map(
        per_device, mesh=mesh, in_specs=in_specs, out_specs=P(None, "leaf", "sub"), check_vma=False
    )
```
